1024 devices in a mesh: blk: 16 (over z, x_lo), group: 64 (over y, x_hi, core).
Axes of the slice: x: 8 (x_hi: 4, x_lo: 2; x = x_hi * 2 + x_lo), y: 8, z: 8, core: 2. Of those that a mesh axis runs over, the one named last changes fastest.
Arguments:
- tokens: bfloat16 [49152, 6, 1152], P(('blk', 'group')), may hold values from -24 to 24
- lengths: int32 [49152], P(('blk', 'group')), may hold values from 1 to 6
- caption_ids: int32 [49152], P(('blk', 'group')), may hold values from 0 to 1023
- destination: int32 [49152], P(('blk', 'group')), may hold values from 0 to 63, as said below
- slot: int32 [49152], P(('blk', 'group')), may hold values from 0 to 1
- images: bfloat16 [131072, 1152], P(('blk', 'group')), may hold values from -24 to 24
- image_ids: int32 [131072], P(('blk', 'group')), may hold values from 0 to 1023
- head_weight: bfloat16 [1152, 1152], replicated, may hold values from -1 to 2
- logit_scale: float32 [1], replicated, may hold values from 4 to 12
- logit_bias: float32 [1], replicated, may hold values from -3 to -1
Outputs:
- image_grad: float32 [131072, 1152], P(('blk', 'group'))
- text_grad: float32 [131072, 1152], P(('blk', 'group'))
- row_loss: float32 [131072], P(('blk', 'group'))
The draws below stay inside these ranges and needn't reach their ends.
Inputs may be any that keep to these rules, and one draw needn't show every extreme that they name: On one device no two captions share a destination and a slot.
All inputs are finite; a program needn't handle non-finite values.
Results may differ from the reference program's by a relative error of at most 0.0044.
Values may be sent and summed in bfloat16 or wider, within the bound.
A program may use at most 64 MiB of HBM per device.

```python
import math
import jax
import jax.numpy as jnp
from jax import lax

D = 1152
L = 6
IMG_DEV = 128
TXT_DEV = 128
CAP_DEV = 48
ID_RANGE = 1024
CAPS = 2
REACH = 4
CAPTIONS = 49152
TEXTS = 131072
IMAGES = 131072
N_BLK = 16
N_GROUP = 64


def route_positions(key):
    devices = CAPTIONS // CAP_DEV
    keys = jax.random.split(key, devices)

    def one_device(device_key):
        order = jax.random.permutation(device_key, TXT_DEV).astype(jnp.int32)
        top_place = jnp.argmax(order == TXT_DEV - 1)
        order = order.at[top_place].set(order[0])
        order = order.at[0].set(TXT_DEV - 1)
        low_place = jnp.argmax(order == 0)
        order = order.at[low_place].set(order[1])
        order = order.at[1].set(0)
        return order[:CAP_DEV]
    return jax.vmap(one_device)(keys).reshape(-1).astype(jnp.int32)


def pair_ids(key, salt_value, row_count):
    pair_list = jax.random.randint(jax.random.fold_in(key, salt_value), (row_count,), 0, ID_RANGE).astype(jnp.int32)
    pair_list = pair_list.at[0].set(ID_RANGE - 1)
    pair_list = pair_list.at[row_count - 1].set(0)
    return pair_list.astype(jnp.int32)


def id_directions(key, shared_weight, own_weight):
    table_key = jax.random.fold_in(key, 5)
    basis_rows = jax.random.normal(jax.random.fold_in(table_key, 1), (8, D), jnp.float32)
    coef_table = jax.random.normal(jax.random.fold_in(table_key, 2), (ID_RANGE, 8), jnp.float32)
    own_part = jax.random.normal(jax.random.fold_in(table_key, 3), (ID_RANGE, D), jnp.float32)
    shared = coef_table[:, 0:1] * basis_rows[0][None, :]
    for member in range(1, 8):
        shared = shared + coef_table[:, member:member + 1] * basis_rows[member][None, :]
    return shared_weight * 8.0 ** (-0.5) * shared + own_weight * own_part


def draw_destination(key, part):
    positions = route_positions(key)
    return (positions // CAPS).astype(jnp.int32)


def draw_slot(key, part):
    positions = route_positions(key)
    return (positions % CAPS).astype(jnp.int32)


def draw_caption_ids(key, part):
    pair_list = pair_ids(key, 12, CAPTIONS)
    return pair_list


def draw_image_ids(key, part):
    pair_list = pair_ids(key, 11, IMAGES)
    return pair_list


def draw_images(key, part):
    pair_list = pair_ids(key, 11, IMAGES)
    table = id_directions(key, 0.8, 0.5)
    key = jax.random.fold_in(key, 21)
    signal = table[pair_list]
    noise = 0.5 * jax.random.normal(jax.random.fold_in(key, 1), (IMAGES, D), jnp.float32)
    return jnp.clip(signal + noise, -24.0, 24.0).astype(jnp.bfloat16)


def draw_tokens(key, part):
    pair_list = pair_ids(key, 12, CAPTIONS)
    table = id_directions(key, 0.8, 0.5)
    key = jax.random.fold_in(key, 22)
    signal = table[pair_list][:, None, :]
    noise = 0.5 * jax.random.normal(jax.random.fold_in(key, 1), (CAPTIONS, L, D), jnp.float32)
    return jnp.clip(signal + noise, -24.0, 24.0).astype(jnp.bfloat16)


def draw_head_weight(key, part):
    key = jax.random.fold_in(key, 31)
    rows = jnp.arange(D, dtype=jnp.int32)
    identity = (rows[:, None] == rows[None, :]).astype(jnp.float32)
    noise = jax.random.normal(key, (D, D), jnp.float32)
    return (identity + 0.5 / math.sqrt(D) * noise).astype(jnp.bfloat16)


def plant(result, stream_key, low, top_value):
    longest = result.shape.index(max(result.shape))
    spots = []
    for shift in (0, 1):
        where = [jax.random.randint(jax.random.fold_in(stream_key, axis), (), 0, length) for axis, length in enumerate(result.shape)]
        where[longest] = (where[longest] + shift) % result.shape[longest]
        spots.append(tuple(where))
    return result.at[spots[0]].set(low).at[spots[1]].set(top_value)


def setup_inputs(seed: int = 0) -> dict:
    key_list = jax.random.split(jax.random.key(seed), 11)
    return {
        "tokens": draw_tokens(jax.random.fold_in(key_list[10], 71), 0),
        "lengths": plant(jax.random.randint(key_list[1], (CAPTIONS,), 1, L + 1), jax.random.fold_in(key_list[1], 1), 1, L).astype(jnp.int32),
        "caption_ids": draw_caption_ids(jax.random.fold_in(key_list[10], 71), 0),
        "destination": draw_destination(jax.random.fold_in(key_list[10], 71), 0),
        "slot": draw_slot(jax.random.fold_in(key_list[10], 71), 0),
        "images": draw_images(jax.random.fold_in(key_list[10], 71), 0),
        "image_ids": draw_image_ids(jax.random.fold_in(key_list[10], 71), 0),
        "head_weight": draw_head_weight(jax.random.fold_in(key_list[10], 71), 0),
        "logit_scale": jnp.clip(jnp.exp(jax.random.uniform(key_list[8], (1,), jnp.float32, math.log(4.0), math.log(12.0))), 4.0, 12.0),
        "logit_bias": jnp.clip(jax.random.uniform(key_list[9], (1,), jnp.float32, -3.0, -1.0), -3.0, -1.0),
    }


NORM_EPS = 1e-06

def pool_block(pair):
    token_block, counts = pair
    live = (jnp.arange(token_block.shape[1], dtype=jnp.int32)[None, :] < counts[:, None]).astype(jnp.float32)
    summed = jnp.einsum('nl,nld->nd', live, token_block.astype(jnp.float32))
    return summed / jnp.maximum(counts, 1).astype(jnp.float32)[:, None]

def reference(tokens, lengths, caption_ids, destination, slot, images, image_ids, head_weight, logit_scale, logit_bias):
    devices = N_BLK * N_GROUP
    pooled_caption = lax.map(pool_block, (tokens.reshape(devices, CAP_DEV, L, D), lengths.reshape(devices, CAP_DEV)))
    pooled_caption = pooled_caption.reshape(CAPTIONS, D)
    owner = jnp.arange(CAPTIONS, dtype=jnp.int32) // CAP_DEV
    target = (owner // N_GROUP * N_GROUP + destination) * TXT_DEV + owner % N_GROUP * CAPS + slot
    target = target.astype(jnp.int32)
    pooled = jnp.zeros((TEXTS, D), jnp.float32).at[target].set(pooled_caption)
    text_ids = jnp.full((TEXTS,), -1, jnp.int32).at[target].set(caption_ids)
    raw = jnp.dot(pooled.astype(jnp.bfloat16), head_weight, preferred_element_type=jnp.float32)
    text_factor = lax.rsqrt(lax.optimization_barrier(jnp.sum(raw * raw, axis=-1, keepdims=True)) + NORM_EPS)
    text_norm = raw * text_factor
    text_b = text_norm.astype(jnp.bfloat16)
    image_f = images.astype(jnp.float32)
    image_factor = lax.rsqrt(lax.optimization_barrier(jnp.sum(image_f * image_f, axis=-1, keepdims=True)) + NORM_EPS)
    image_norm = image_f * image_factor
    image_b = image_norm.astype(jnp.bfloat16)
    image_four = image_b.reshape(N_BLK, N_GROUP, IMG_DEV, D).astype(jnp.float32)
    image_idfour = image_ids.reshape(N_BLK, N_GROUP, IMG_DEV)
    text_four = text_b.reshape(N_BLK, N_GROUP, TXT_DEV, D)
    text_idfour = text_ids.reshape(N_BLK, N_GROUP, TXT_DEV)
    scale_value = logit_scale[0]
    bias_value = logit_bias[0]
    image_sum = jnp.zeros((N_BLK, N_GROUP, IMG_DEV, D), jnp.float32)
    text_sum = jnp.zeros((N_BLK, N_GROUP, TXT_DEV, D), jnp.float32)
    loss_rows = jnp.zeros((N_BLK, N_GROUP, IMG_DEV), jnp.float32)
    for offset in range(-REACH, REACH + 1):
        blocks = jnp.roll(text_four, -offset, axis=0).astype(jnp.float32)
        block_ids = jnp.roll(text_idfour, -offset, axis=0)
        products = jnp.einsum('bgid,bgjd->bgij', image_four, blocks)
        logits = scale_value * products + bias_value
        signs = jnp.where(image_idfour[..., :, None] == block_ids[..., None, :], 1.0, -1.0).astype(jnp.float32)
        live = (block_ids >= 0).astype(jnp.float32)[..., None, :]
        loss_rows = loss_rows + lax.optimization_barrier(jnp.sum(live * jax.nn.softplus(-signs * logits), axis=-1))
        weights = (live * -signs * jax.nn.sigmoid(-signs * logits) * scale_value).astype(jnp.bfloat16).astype(jnp.float32)
        image_sum = image_sum + jnp.einsum('bgij,bgjd->bgid', weights, blocks)
        partial_sum = jnp.einsum('bgij,bgid->bgjd', weights, image_four)
        text_sum = text_sum + jnp.roll(partial_sum, offset, axis=0)
    image_sum = image_sum.reshape(IMAGES, D)
    text_sum = text_sum.reshape(TEXTS, D)
    image_grad = image_factor * (image_sum - image_norm * lax.optimization_barrier(jnp.sum(image_norm * image_sum, axis=-1, keepdims=True)))
    text_raw_grad = text_factor * (text_sum - text_norm * lax.optimization_barrier(jnp.sum(text_norm * text_sum, axis=-1, keepdims=True)))
    text_grad = lax.dot_general(text_raw_grad.astype(jnp.bfloat16), head_weight, (((1,), (1,)), ((), ())), preferred_element_type=jnp.float32)
    return (image_grad, text_grad, loss_rows.reshape(IMAGES))
```

```python
import jax
import jax.numpy as jnp
from jax import lax
from jax.experimental import pallas as pl
from jax.experimental.pallas import tpu as pltpu
from jax.sharding import PartitionSpec as P

D = 1152
ROWS = 128
CAPS_HERE = 48
TOKENS = 6
NORM_EPS = 1e-06
HALF = 640
FAN = 8
PIECES = 2
PIECE = ROWS // PIECES
MESH = pl.DeviceIdType.MESH
BF16 = jnp.bfloat16
F32 = jnp.float32


def iota(shape, dim):
    return lax.broadcasted_iota(jnp.int32, shape, dim)


def dot(a, b):
    return lax.dot_general(a, b, (((1,), (0,)), ((), ())), preferred_element_type=F32)


def dot_t(a, b):
    return lax.dot_general(a, b, (((1,), (1,)), ((), ())), preferred_element_type=F32)


def swap_pairs(r):
    return ((r >> 1) & 7) * 16 + (r >> 4) * 2 + (r & 1)


def kernel(
    tokens_hbm,
    lengths_hbm,
    caption_ids_hbm,
    destination_hbm,
    slot_hbm,
    images_hbm,
    image_ids_hbm,
    head_hbm,
    scale_ref,
    bias_ref,
    image_grad_hbm,
    text_grad_hbm,
    loss_hbm,
    tokens,
    meta,
    images,
    image_ids_in,
    head,
    out_image,
    out_text,
    out_loss,
    im_buf,
    im_ids,
    im_peer,
    im_peer_ids,
    tx_buf,
    tx_ids,
    tx_peer,
    tx_peer_ids,
    send_a1,
    recv_a1,
    send_a2,
    recv_a2,
    send_b1,
    recv_b1,
    send_b2,
    recv_b2,
    raw_ref,
    sum_own,
    sum_peer,
    text_sum,
    txp_out,
    txp_in,
    imp_out,
    imp_in,
    lossp_out,
    lossp_in,
    in_sem,
    out_sem,
    swap_send,
    swap_recv,
    z_send,
    z_recv,
    zid_send,
    zid_recv,
    x_send,
    x_recv,
):
    blk = lax.axis_index("blk")
    grp = lax.axis_index("group")
    col = blk % 2
    peer = {"blk": blk + 1 - 2 * col}
    up = {"blk": (blk + 2) % 16}
    down = {"blk": (blk + 14) % 16}
    y, u = grp // FAN, grp % FAN
    y_peer = [{"group": ((y + k) % FAN) * FAN + u} for k in range(FAN)]
    u_peer = [{"group": y * FAN + (u + k) % FAN} for k in range(FAN)]

    loads = [
        pltpu.make_async_copy(src, dst, in_sem.at[i])
        for i, (src, dst) in enumerate(
            [
                (images_hbm, images),
                (image_ids_hbm, image_ids_in),
                (lengths_hbm, meta.at[0]),
                (destination_hbm, meta.at[1]),
                (slot_hbm, meta.at[2]),
                (caption_ids_hbm, meta.at[3]),
                (tokens_hbm, tokens),
                (head_hbm, head),
            ]
        )
    ]
    for load in loads:
        load.start()

    barrier = pltpu.get_barrier_semaphore()
    greeted = [peer, up, down] + y_peer[1:] + u_peer[1:]
    for other in greeted:
        pl.semaphore_signal(barrier, inc=1, device_id=other, device_id_type=MESH)

    def remote(src, dst, send, recv, to):
        return pltpu.make_async_remote_copy(
            src_ref=src, dst_ref=dst, send_sem=send, recv_sem=recv, device_id=to, device_id_type=MESH
        )

    loads[0].wait()
    loads[1].wait()
    image_f = images[...].astype(F32)
    image_factor = lax.rsqrt(jnp.sum(image_f * image_f, axis=1, keepdims=True) + NORM_EPS)
    im_buf[0:ROWS, :] = (image_f * image_factor).astype(BF16)
    im_ids[0] = jnp.broadcast_to(image_ids_in[...].astype(F32), (8, ROWS))

    for i in range(2, 6):
        loads[i].wait()
    lengths = meta[0]
    position = meta[1] * 2 + meta[2]
    places = 288
    spread = iota((CAPS_HERE, places), 1) - iota((CAPS_HERE, places), 0)
    hit = spread == 0
    level = jnp.zeros((1, places), jnp.int32)
    lane = iota((1, places), 1)
    for step in range(1, TOKENS):
        hit = hit | (spread == CAPS_HERE * step)
        level = level + (lane >= CAPS_HERE * step).astype(jnp.int32)
    spread_b = hit.astype(F32).astype(BF16)
    wide_length = dot(jnp.broadcast_to(lengths, (16, CAPS_HERE)).astype(F32).astype(BF16), spread_b)[0:1, :]
    wide_position = dot(jnp.broadcast_to(position, (16, CAPS_HERE)).astype(F32).astype(BF16), spread_b)[0:1, :]
    wide_position = jnp.where(level.astype(F32) < wide_length, wide_position, -1.0)

    def row_slot(r):
        return ((y + (r >> 4)) % FAN) * 16 + ((u + ((r >> 1) & 7)) % FAN) * 2 + (r & 1)

    def gather_matrix(order):
        return (order.astype(F32) == wide_position).astype(F32).astype(BF16)

    def own_captions(order):
        return order == position

    loads[6].wait()
    order_a = row_slot(iota((ROWS, 1), 0))
    order_b = row_slot(swap_pairs(iota((ROWS, 1), 0)))
    here_a = own_captions(order_a)
    here_b = own_captions(order_b)
    count_a = jnp.sum(jnp.where(here_a, lengths, 0).astype(F32), axis=1, keepdims=True)
    count_b = jnp.sum(jnp.where(here_b, lengths, 0).astype(F32), axis=1, keepdims=True)
    ids_b = jnp.sum(jnp.where(here_b, meta[3] + 1, 0).astype(F32), axis=1, keepdims=True).astype(jnp.int32)
    send_a1[...] = (dot(gather_matrix(order_a), tokens[:, 0:HALF]) / jnp.maximum(count_a, 1.0)).astype(BF16)
    send_b1[:, 0 : D - HALF] = (
        dot(gather_matrix(order_b), tokens[:, HALF:D]) / jnp.maximum(count_b, 1.0)
    ).astype(BF16)
    id_lane = iota((ROWS, ROWS), 1)
    send_b1[:, D - HALF : HALF] = (
        jnp.where(id_lane == 0, ids_b >> 5, jnp.where(id_lane == 1, ids_b & 31, 0)).astype(F32).astype(BF16)
    )

    pl.semaphore_wait(barrier, len(greeted))

    def swap(stage, src, dst, to):
        copies = []
        for k in range(1, FAN):
            copy = remote(
                src.at[pl.ds(k * 16, 16)],
                dst.at[pl.ds(k * 16, 16)],
                swap_send.at[stage, k],
                swap_recv.at[stage, k],
                to[k],
            )
            copy.start()
            copies.append(copy)
        dst[0:16, :] = src[0:16, :]
        return copies

    def own_along_z(kind, buf, ids):
        copies = []
        for way, (to, place) in enumerate(((up, 1), (down, 2))):
            tag = zid_send.at[kind, place], zid_recv.at[kind, place]
            copies.append(remote(ids.at[0], ids.at[place], *tag, to))
        for piece in range(PIECES):
            for way, (to, place) in enumerate(((up, 1), (down, 2))):
                copies.append(
                    remote(
                        buf.at[pl.ds(piece * PIECE, PIECE)],
                        buf.at[pl.ds(place * ROWS + piece * PIECE, PIECE)],
                        z_send.at[kind, place, piece],
                        z_recv.at[kind, place, piece],
                        to,
                    )
                )
        for copy in copies:
            copy.start()
        return copies

    def pass_along_z(kind, buf, ids, arriving):
        copies = []
        for way, (to, place) in enumerate(((up, 1), (down, 2))):
            arriving[way].wait_recv()
            far = place + 2
            copy = remote(
                ids.at[place], ids.at[far], zid_send.at[kind, far], zid_recv.at[kind, far], to
            )
            copy.start()
            copies.append(copy)
        for piece in range(PIECES):
            for way, (to, place) in enumerate(((up, 1), (down, 2))):
                arriving[2 + piece * 2 + way].wait_recv()
                far = place + 2
                copy = remote(
                    buf.at[pl.ds(place * ROWS + piece * PIECE, PIECE)],
                    buf.at[pl.ds(far * ROWS + piece * PIECE, PIECE)],
                    z_send.at[kind, far, piece],
                    z_recv.at[kind, far, piece],
                    to,
                )
                copy.start()
                copies.append(copy)
        return copies

    def to_peer(i, src, dst):
        copy = remote(src, dst, x_send.at[i], x_recv.at[i], peer)
        copy.start()
        return copy

    sent = []
    swap_a1 = swap(0, send_a1, recv_a1, y_peer)
    swap_b1 = swap(1, send_b1, recv_b1, u_peer)
    im_near = own_along_z(0, im_buf, im_ids)
    im_x = [to_peer(0, im_buf.at[pl.ds(0, ROWS)], im_peer), to_peer(1, im_ids.at[0], im_peer_ids)]

    r_out = iota((ROWS, ROWS), 0)
    r_in = iota((ROWS, ROWS), 1)
    turn = (swap_pairs(r_out) == r_in).astype(F32).astype(BF16)
    for copy in swap_a1:
        copy.wait_recv()
    send_a2[...] = dot(turn, recv_a1[...]).astype(BF16)
    swap_a2 = swap(2, send_a2, recv_a2, u_peer)
    for copy in swap_b1:
        copy.wait_recv()
    send_b2[...] = dot(turn, recv_b1[...]).astype(BF16)
    swap_b2 = swap(3, send_b2, recv_b2, y_peer)

    im_far = pass_along_z(0, im_buf, im_ids, im_near)

    def home_slot(r):
        return ((y + FAN - (r >> 4)) % FAN) * 16 + ((u + FAN - ((r >> 1) & 7)) % FAN) * 2 + (r & 1)

    for copy in swap_a2:
        copy.wait_recv()
    home_a = (home_slot(swap_pairs(r_in)) == r_out).astype(F32).astype(BF16)
    pooled_a = dot(home_a, recv_a2[...]).astype(BF16)
    loads[7].wait()
    raw_a = dot(pooled_a, head[0:HALF, :])
    for copy in swap_b2:
        copy.wait_recv()
    home_b = (home_slot(r_in) == r_out).astype(F32).astype(BF16)
    pooled_b = dot(home_b, recv_b2[...]).astype(BF16)
    raw = raw_a + dot(pooled_b[:, 0 : D - HALF], head[HALF:D, :])
    raw_ref[...] = raw
    text_factor = lax.rsqrt(jnp.sum(raw * raw, axis=1, keepdims=True) + NORM_EPS)
    tx_buf[0:ROWS, :] = (raw * text_factor).astype(BF16)
    id_codes = pooled_b[:, D - HALF : HALF]
    weigh_in = jnp.where(r_in == 0, 32.0, jnp.where(r_in == 1, 1.0, 0.0)).astype(BF16)
    tx_cols = dot_t(weigh_in, id_codes) - 1.0
    tx_ids[0] = tx_cols[0:8, :]
    tx_near = own_along_z(1, tx_buf, tx_ids)
    tx_x = [to_peer(2, tx_buf.at[pl.ds(0, ROWS)], tx_peer), to_peer(3, tx_ids.at[0], tx_peer_ids)]

    scale = scale_ref[0]
    bias = bias_ref[0]

    def as_rows(ids):
        return jnp.transpose(jnp.broadcast_to(ids, (ROWS, ROWS)))

    def terms(rows, row_ids, cols, col_ids, text_is_rows, far_masks):
        logits = scale * dot_t(rows, cols) + bias
        blocks = len(col_ids)
        wide_cols = jnp.concatenate(col_ids, axis=1)
        wide_rows = jnp.concatenate([row_ids] * blocks, axis=1)
        same = wide_rows == wide_cols
        live = ((wide_rows if text_is_rows else wide_cols) >= 0.0).astype(F32)
        if far_masks is not None:
            ones = jnp.ones((1, ROWS), F32)
            allowed = jnp.concatenate(
                [ones] * (blocks - 2) + [ones * far_masks[0], ones * far_masks[1]], axis=1
            )
            live = live * allowed
        flipped = jnp.where(same, -logits, logits)
        small = jnp.exp(-jnp.abs(flipped))
        sigmoid = jnp.where(flipped >= 0.0, 1.0, small) / (1.0 + small)
        weights = (live * jnp.where(same, -scale, scale) * sigmoid).astype(BF16)
        if text_is_rows:
            return weights, None
        softplus = jnp.maximum(flipped, 0.0) + jnp.log1p(small)
        return weights, jnp.sum(live * softplus, axis=1, keepdims=True)

    col_f = col.astype(F32)
    far_masks = (col_f, 1.0 - col_f)

    for copy in im_far:
        copy.wait_recv()
    im_cols = [im_ids[place][0:1, :] for place in range(5)]
    weights, _ = terms(tx_buf[0:ROWS, :], as_rows(tx_cols[0:1, :]), im_buf[...], im_cols, True, None)
    text_sum[...] = dot(weights, im_buf[...])

    for copy in im_x:
        copy.wait_recv()
    own_rows = as_rows(im_ids[0][0:1, :])
    peer_rows = as_rows(im_peer_ids[0:1, :])

    tx_far = pass_along_z(1, tx_buf, tx_ids, tx_near)

    for copy in tx_x:
        copy.wait_recv()
    weights, _ = terms(tx_peer[...], as_rows(tx_peer_ids[0:1, :]), im_buf[...], im_cols, True, far_masks)
    txp_out[...] = dot(weights, im_buf[...]).astype(BF16)
    txp = to_peer(4, txp_out, txp_in)

    def image_terms(rows, row_ids, place, blocks, masks):
        cols = tx_buf[place * ROWS : (place + blocks) * ROWS, :]
        ids = [tx_ids[p][0:1, :] for p in range(place, place + blocks)]
        weights, loss = terms(rows, row_ids, cols, ids, False, masks)
        return dot(weights, cols), loss

    own_im = im_buf[0:ROWS, :]
    part, loss_own = image_terms(own_im, own_rows, 0, 3, None)
    sum_own[...] = part
    part, loss_peer = image_terms(im_peer[...], peer_rows, 0, 3, None)
    sum_peer[...] = part

    for copy in tx_far:
        copy.wait_recv()
    part, loss = image_terms(im_peer[...], peer_rows, 3, 2, far_masks)
    imp_out[...] = (sum_peer[...] + part).astype(BF16)
    loss_peer = loss_peer + loss
    lossp_out[...] = jnp.transpose(jnp.broadcast_to(loss_peer, (ROWS, ROWS)))[0:8, :]
    imp = [to_peer(5, imp_out, imp_in), to_peer(6, lossp_out, lossp_in)]
    part, loss = image_terms(own_im, own_rows, 3, 2, None)
    sum_own[...] += part
    loss_own = loss_own + loss
    loss_row = jnp.transpose(jnp.broadcast_to(loss_own, (ROWS, ROWS)))[0:1, :]

    txp.wait_recv()
    total = text_sum[...] + txp_in[...].astype(F32)
    text_norm = raw_ref[...] * text_factor
    along = jnp.sum(text_norm * total, axis=1, keepdims=True)
    text_raw_grad = (text_factor * (total - text_norm * along)).astype(BF16)
    out_text[...] = dot_t(text_raw_grad, head[...])
    store_text = pltpu.make_async_copy(out_text, text_grad_hbm, out_sem.at[0])
    store_text.start()

    for copy in imp:
        copy.wait_recv()
    out_loss[...] = loss_row + lossp_in[0:1, :]
    store_loss = pltpu.make_async_copy(out_loss, loss_hbm, out_sem.at[1])
    store_loss.start()
    total = sum_own[...] + imp_in[...].astype(F32)
    image_norm = images[...].astype(F32) * image_factor
    along = jnp.sum(image_norm * total, axis=1, keepdims=True)
    out_image[...] = image_factor * (total - image_norm * along)
    store_image = pltpu.make_async_copy(out_image, image_grad_hbm, out_sem.at[2])
    store_image.start()

    for copy in swap_a1 + swap_b1 + swap_a2 + swap_b2 + im_near + im_far + im_x + tx_near + tx_far + tx_x:
        copy.wait_send()
    for copy in [txp] + imp:
        copy.wait_send()
    store_text.wait()
    store_loss.wait()
    store_image.wait()


def per_device(
    tokens, lengths, caption_ids, destination, slot, images, image_ids, head_weight, logit_scale, logit_bias
):
    any_spec = pl.BlockSpec(memory_space=pl.ANY)
    smem_spec = pl.BlockSpec(memory_space=pltpu.SMEM)

    def vmem(shape, dtype):
        return pltpu.VMEM(shape, dtype)

    block = (ROWS, D)
    flat_tokens = jnp.transpose(tokens, (1, 0, 2)).reshape(TOKENS * CAPS_HERE, D)
    as_row = lambda a: a.reshape(1, a.shape[0])
    image_grad, text_grad, loss = pl.pallas_call(
        kernel,
        out_shape=(
            jax.ShapeDtypeStruct(block, F32),
            jax.ShapeDtypeStruct(block, F32),
            jax.ShapeDtypeStruct((1, ROWS), F32),
        ),
        in_specs=[any_spec] * 8 + [smem_spec] * 2,
        out_specs=(any_spec, any_spec, any_spec),
        scratch_shapes=[
            vmem((TOKENS * CAPS_HERE, D), BF16),
            vmem((4, 1, CAPS_HERE), jnp.int32),
            vmem(block, BF16),
            vmem((1, ROWS), jnp.int32),
            vmem((D, D), BF16),
            vmem(block, F32),
            vmem(block, F32),
            vmem((1, ROWS), F32),
            vmem((5 * ROWS, D), BF16),
            vmem((5, 8, ROWS), F32),
            vmem(block, BF16),
            vmem((8, ROWS), F32),
            vmem((5 * ROWS, D), BF16),
            vmem((5, 8, ROWS), F32),
            vmem(block, BF16),
            vmem((8, ROWS), F32),
        ]
        + [vmem((ROWS, HALF), BF16)] * 8
        + [
            vmem(block, F32),
            vmem(block, F32),
            vmem(block, F32),
            vmem(block, F32),
            vmem(block, BF16),
            vmem(block, BF16),
            vmem(block, BF16),
            vmem(block, BF16),
            vmem((8, ROWS), F32),
            vmem((8, ROWS), F32),
            pltpu.SemaphoreType.DMA((8,)),
            pltpu.SemaphoreType.DMA((3,)),
            pltpu.SemaphoreType.DMA((4, FAN)),
            pltpu.SemaphoreType.DMA((4, FAN)),
            pltpu.SemaphoreType.DMA((2, 5, PIECES)),
            pltpu.SemaphoreType.DMA((2, 5, PIECES)),
            pltpu.SemaphoreType.DMA((2, 5)),
            pltpu.SemaphoreType.DMA((2, 5)),
            pltpu.SemaphoreType.DMA((7,)),
            pltpu.SemaphoreType.DMA((7,)),
        ],
        compiler_params=pltpu.CompilerParams(
            collective_id=0, has_side_effects=True, vmem_limit_bytes=40 * 1024 * 1024
        ),
        name="band",
    )(
        flat_tokens,
        as_row(lengths),
        as_row(caption_ids),
        as_row(destination),
        as_row(slot),
        images,
        as_row(image_ids),
        head_weight,
        logit_scale,
        logit_bias,
    )
    return (image_grad, text_grad, loss.reshape(ROWS))


def solution(mesh):
    spec1 = P(("blk", "group"))
    spec2 = P(("blk", "group"), None)
    return jax.shard_map(
        per_device,
        mesh=mesh,
        in_specs=(
            P(("blk", "group"), None, None),
            spec1,
            spec1,
            spec1,
            spec1,
            spec2,
            spec1,
            P(None, None),
            P(None),
            P(None),
        ),
        out_specs=(spec2, spec2, spec1),
        check_vma=False,
    )
```

```python
import jax
import jax.numpy as jnp
from jax import lax
from jax.experimental import pallas as pl
from jax.experimental.pallas import tpu as pltpu
from jax.sharding import PartitionSpec as P

D = 1152
ROWS = 128
CAPS_HERE = 48
TOKENS = 6
NORM_EPS = 1e-06
HALF = 640
FAN = 8
PIECES = 2
PIECE = ROWS // PIECES
EARLY = 32
HALF_ROWS = ROWS // 2
MESH = pl.DeviceIdType.MESH
BF16 = jnp.bfloat16
F32 = jnp.float32


def iota(shape, dim):
    return lax.broadcasted_iota(jnp.int32, shape, dim)


def dot(a, b):
    return lax.dot_general(a, b, (((1,), (0,)), ((), ())), preferred_element_type=F32)


def dot_t(a, b):
    return lax.dot_general(a, b, (((1,), (1,)), ((), ())), preferred_element_type=F32)


def swap_pairs(r):
    return ((r >> 1) & 7) * 16 + (r >> 4) * 2 + (r & 1)


def kernel(
    tokens_hbm,
    lengths_hbm,
    caption_ids_hbm,
    destination_hbm,
    slot_hbm,
    images_hbm,
    image_ids_hbm,
    head_hbm,
    scale_ref,
    bias_ref,
    out_image,
    out_text,
    out_loss,
    tokens,
    meta,
    images,
    image_ids_in,
    head,
    im_buf,
    im_ids,
    im_peer,
    im_peer_ids,
    tx_buf,
    tx_ids,
    tx_peer,
    tx_peer_ids,
    send_a1,
    recv_a1,
    send_a2,
    recv_a2,
    send_b1,
    recv_b1,
    send_b2,
    recv_b2,
    raw_ref,
    sum_own,
    sum_peer,
    text_sum,
    txp_out,
    txp_in,
    imp_out,
    imp_in,
    lossp_out,
    lossp_in,
    in_sem,
    swap_send,
    swap_recv,
    z_send,
    z_recv,
    zid_send,
    zid_recv,
    x_send,
    x_recv,
):
    blk = lax.axis_index("blk")
    grp = lax.axis_index("group")
    col = blk % 2
    peer = {"blk": blk + 1 - 2 * col}
    up = {"blk": (blk + 2) % 16}
    down = {"blk": (blk + 14) % 16}
    y, u = grp // FAN, grp % FAN
    y_peer = [{"group": ((y + k) % FAN) * FAN + u} for k in range(FAN)]
    u_peer = [{"group": y * FAN + (u + k) % FAN} for k in range(FAN)]

    loads = [
        pltpu.make_async_copy(src, dst, in_sem.at[i])
        for i, (src, dst) in enumerate(
            [
                (images_hbm, images),
                (image_ids_hbm, image_ids_in),
                (lengths_hbm, meta.at[0]),
                (destination_hbm, meta.at[1]),
                (slot_hbm, meta.at[2]),
                (caption_ids_hbm, meta.at[3]),
                (tokens_hbm, tokens),
                (head_hbm, head),
            ]
        )
    ]
    for load in loads:
        load.start()

    barrier = pltpu.get_barrier_semaphore()
    greeted = [peer, up, down] + y_peer[1:] + u_peer[1:]
    for other in greeted:
        pl.semaphore_signal(barrier, inc=1, device_id=other, device_id_type=MESH)

    def remote(src, dst, send, recv, to):
        return pltpu.make_async_remote_copy(
            src_ref=src, dst_ref=dst, send_sem=send, recv_sem=recv, device_id=to, device_id_type=MESH
        )

    loads[0].wait()
    loads[1].wait()
    image_f = images[...].astype(F32)
    image_factor = lax.rsqrt(jnp.sum(image_f * image_f, axis=1, keepdims=True) + NORM_EPS)
    im_buf[0:ROWS, :] = (image_f * image_factor).astype(BF16)
    im_ids[0] = jnp.broadcast_to(image_ids_in[...].astype(F32), (8, ROWS))

    for i in range(2, 6):
        loads[i].wait()
    lengths = meta[0]
    position = meta[1] * 2 + meta[2]
    places = 288
    spread = iota((CAPS_HERE, places), 1) - iota((CAPS_HERE, places), 0)
    hit = spread == 0
    level = jnp.zeros((1, places), jnp.int32)
    lane = iota((1, places), 1)
    for step in range(1, TOKENS):
        hit = hit | (spread == CAPS_HERE * step)
        level = level + (lane >= CAPS_HERE * step).astype(jnp.int32)
    spread_b = hit.astype(F32).astype(BF16)
    wide_length = dot(jnp.broadcast_to(lengths, (16, CAPS_HERE)).astype(F32).astype(BF16), spread_b)[0:1, :]
    wide_position = dot(jnp.broadcast_to(position, (16, CAPS_HERE)).astype(F32).astype(BF16), spread_b)[0:1, :]
    wide_position = jnp.where(level.astype(F32) < wide_length, wide_position, -1.0)

    def row_slot(r):
        return ((y + (r >> 4)) % FAN) * 16 + ((u + ((r >> 1) & 7)) % FAN) * 2 + (r & 1)

    def gather_matrix(order):
        return (order.astype(F32) == wide_position).astype(F32).astype(BF16)

    def own_captions(order):
        return order == position

    loads[6].wait()
    order_a = row_slot(iota((ROWS, 1), 0))
    order_b = row_slot(swap_pairs(iota((ROWS, 1), 0)))
    here_a = own_captions(order_a)
    here_b = own_captions(order_b)
    count_a = jnp.sum(jnp.where(here_a, lengths, 0).astype(F32), axis=1, keepdims=True)
    count_b = jnp.sum(jnp.where(here_b, lengths, 0).astype(F32), axis=1, keepdims=True)
    ids_b = jnp.sum(jnp.where(here_b, meta[3] + 1, 0).astype(F32), axis=1, keepdims=True).astype(jnp.int32)
    send_a1[...] = (dot(gather_matrix(order_a), tokens[:, 0:HALF]) / jnp.maximum(count_a, 1.0)).astype(BF16)
    send_b1[:, 0 : D - HALF] = (
        dot(gather_matrix(order_b), tokens[:, HALF:D]) / jnp.maximum(count_b, 1.0)
    ).astype(BF16)
    id_lane = iota((ROWS, ROWS), 1)
    send_b1[:, D - HALF : HALF] = (
        jnp.where(id_lane == 0, ids_b >> 5, jnp.where(id_lane == 1, ids_b & 31, 0)).astype(F32).astype(BF16)
    )

    pl.semaphore_wait(barrier, len(greeted))

    def swap(stage, src, dst, to):
        copies = []
        for k in range(1, FAN):
            copy = remote(
                src.at[pl.ds(k * 16, 16)],
                dst.at[pl.ds(k * 16, 16)],
                swap_send.at[stage, k],
                swap_recv.at[stage, k],
                to[k],
            )
            copy.start()
            copies.append(copy)
        dst[0:16, :] = src[0:16, :]
        return copies

    def own_along_z(kind, buf, ids):
        copies = []
        for way, (to, place) in enumerate(((up, 1), (down, 2))):
            tag = zid_send.at[kind, place], zid_recv.at[kind, place]
            copies.append(remote(ids.at[0], ids.at[place], *tag, to))
        for piece in range(PIECES):
            for way, (to, place) in enumerate(((up, 1), (down, 2))):
                copies.append(
                    remote(
                        buf.at[pl.ds(piece * PIECE, PIECE)],
                        buf.at[pl.ds(place * ROWS + piece * PIECE, PIECE)],
                        z_send.at[kind, place, piece],
                        z_recv.at[kind, place, piece],
                        to,
                    )
                )
        for copy in copies:
            copy.start()
        return copies

    def pass_along_z(kind, buf, ids, arriving):
        copies = []
        for way, (to, place) in enumerate(((up, 1), (down, 2))):
            arriving[way].wait_recv()
            far = place + 2
            copy = remote(
                ids.at[place], ids.at[far], zid_send.at[kind, far], zid_recv.at[kind, far], to
            )
            copy.start()
            copies.append(copy)
        for piece in range(PIECES):
            for way, (to, place) in enumerate(((up, 1), (down, 2))):
                arriving[2 + piece * 2 + way].wait_recv()
                far = place + 2
                copy = remote(
                    buf.at[pl.ds(place * ROWS + piece * PIECE, PIECE)],
                    buf.at[pl.ds(far * ROWS + piece * PIECE, PIECE)],
                    z_send.at[kind, far, piece],
                    z_recv.at[kind, far, piece],
                    to,
                )
                copy.start()
                copies.append(copy)
        return copies

    def to_peer(i, src, dst):
        copy = remote(src, dst, x_send.at[i], x_recv.at[i], peer)
        copy.start()
        return copy

    sent = []
    swap_a1 = swap(0, send_a1, recv_a1, y_peer)
    swap_b1 = swap(1, send_b1, recv_b1, u_peer)
    im_near = own_along_z(0, im_buf, im_ids)
    im_x = [
        to_peer(0, im_buf.at[pl.ds(0, EARLY)], im_peer.at[pl.ds(0, EARLY)]),
        to_peer(1, im_ids.at[0], im_peer_ids),
    ]

    r_out = iota((ROWS, ROWS), 0)
    r_in = iota((ROWS, ROWS), 1)
    turn = (swap_pairs(r_out) == r_in).astype(F32).astype(BF16)
    for copy in swap_a1:
        copy.wait_recv()
    send_a2[...] = dot(turn, recv_a1[...]).astype(BF16)
    swap_a2 = swap(2, send_a2, recv_a2, u_peer)
    im_x.append(to_peer(7, im_buf.at[pl.ds(EARLY, ROWS - EARLY)], im_peer.at[pl.ds(EARLY, ROWS - EARLY)]))
    for copy in swap_b1:
        copy.wait_recv()
    send_b2[...] = dot(turn, recv_b1[...]).astype(BF16)
    swap_b2 = swap(3, send_b2, recv_b2, y_peer)

    im_far = pass_along_z(0, im_buf, im_ids, im_near)

    def home_slot(r):
        return ((y + FAN - (r >> 4)) % FAN) * 16 + ((u + FAN - ((r >> 1) & 7)) % FAN) * 2 + (r & 1)

    for copy in swap_a2:
        copy.wait_recv()
    home_a = (home_slot(swap_pairs(r_in)) == r_out).astype(F32).astype(BF16)
    pooled_a = dot(home_a, recv_a2[...]).astype(BF16)
    loads[7].wait()
    raw_a = dot(pooled_a, head[0:HALF, :])
    for copy in swap_b2:
        copy.wait_recv()
    home_b = (home_slot(r_in) == r_out).astype(F32).astype(BF16)
    pooled_b = dot(home_b, recv_b2[...]).astype(BF16)
    raw = raw_a + dot(pooled_b[:, 0 : D - HALF], head[HALF:D, :])
    raw_ref[...] = raw
    text_factor = lax.rsqrt(jnp.sum(raw * raw, axis=1, keepdims=True) + NORM_EPS)
    tx_buf[0:ROWS, :] = (raw * text_factor).astype(BF16)
    id_codes = pooled_b[:, D - HALF : HALF]
    weigh_in = jnp.where(r_in == 0, 32.0, jnp.where(r_in == 1, 1.0, 0.0)).astype(BF16)
    tx_cols = dot_t(weigh_in, id_codes) - 1.0
    tx_ids[0] = tx_cols[0:8, :]
    tx_near = own_along_z(1, tx_buf, tx_ids)
    tx_x = [to_peer(2, tx_buf.at[pl.ds(0, ROWS)], tx_peer), to_peer(3, tx_ids.at[0], tx_peer_ids)]

    scale = scale_ref[0]
    bias = bias_ref[0]

    def as_rows(ids):
        return jnp.transpose(jnp.broadcast_to(ids, (ROWS, ROWS)))

    def terms(rows, row_ids, cols, col_ids, text_is_rows, far_masks):
        logits = scale * dot_t(rows, cols) + bias
        blocks = len(col_ids)
        wide_cols = jnp.concatenate(col_ids, axis=1)
        wide_rows = jnp.concatenate([row_ids] * blocks, axis=1)
        same = wide_rows == wide_cols
        live = ((wide_rows if text_is_rows else wide_cols) >= 0.0).astype(F32)
        if far_masks is not None:
            ones = jnp.ones((1, ROWS), F32)
            allowed = jnp.concatenate(
                [ones] * (blocks - 2) + [ones * far_masks[0], ones * far_masks[1]], axis=1
            )
            live = live * allowed
        flipped = jnp.where(same, -logits, logits)
        small = jnp.exp(-jnp.abs(flipped))
        sigmoid = jnp.where(flipped >= 0.0, 1.0, small) / (1.0 + small)
        weights = (live * jnp.where(same, -scale, scale) * sigmoid).astype(BF16)
        if text_is_rows:
            return weights, None
        softplus = jnp.maximum(flipped, 0.0) + jnp.log1p(small)
        return weights, jnp.sum(live * softplus, axis=1, keepdims=True)

    col_f = col.astype(F32)
    far_masks = (col_f, 1.0 - col_f)

    for copy in im_far:
        copy.wait_recv()
    im_cols = [im_ids[place][0:1, :] for place in range(5)]
    weights, _ = terms(tx_buf[0:ROWS, :], as_rows(tx_cols[0:1, :]), im_buf[...], im_cols, True, None)
    text_sum[...] = dot(weights, im_buf[...])

    for copy in im_x:
        copy.wait_recv()
    own_rows = as_rows(im_ids[0][0:1, :])
    peer_rows = as_rows(im_peer_ids[0:1, :])

    tx_far = pass_along_z(1, tx_buf, tx_ids, tx_near)

    for copy in tx_x:
        copy.wait_recv()
    weights, _ = terms(tx_peer[...], as_rows(tx_peer_ids[0:1, :]), im_buf[...], im_cols, True, far_masks)
    txp_out[...] = dot(weights, im_buf[...]).astype(BF16)
    txp = to_peer(4, txp_out, txp_in)

    def image_terms(rows, row_ids, place, blocks, masks):
        cols = tx_buf[place * ROWS : (place + blocks) * ROWS, :]
        ids = [tx_ids[p][0:1, :] for p in range(place, place + blocks)]
        weights, loss = terms(rows, row_ids, cols, ids, False, masks)
        return dot(weights, cols), loss

    own_im = im_buf[0:ROWS, :]
    part, loss_own = image_terms(own_im, own_rows, 0, 3, None)
    sum_own[...] = part
    part, loss_peer = image_terms(im_peer[...], peer_rows, 0, 3, None)
    sum_peer[...] = part

    for copy in tx_far:
        copy.wait_recv()
    part, loss = image_terms(im_peer[...], peer_rows, 3, 2, far_masks)
    imp_out[...] = (sum_peer[...] + part).astype(BF16)
    loss_peer = loss_peer + loss
    lossp_out[...] = jnp.transpose(jnp.broadcast_to(loss_peer, (ROWS, ROWS)))[0:8, :]
    imp = [
        to_peer(6, lossp_out, lossp_in),
        to_peer(5, imp_out.at[pl.ds(0, HALF_ROWS)], imp_in.at[pl.ds(0, HALF_ROWS)]),
        to_peer(8, imp_out.at[pl.ds(HALF_ROWS, HALF_ROWS)], imp_in.at[pl.ds(HALF_ROWS, HALF_ROWS)]),
    ]
    part, loss = image_terms(own_im, own_rows, 3, 2, None)
    sum_own[...] += part
    loss_own = loss_own + loss
    loss_row = jnp.transpose(jnp.broadcast_to(loss_own, (ROWS, ROWS)))[0:1, :]

    txp.wait_recv()
    total = text_sum[...] + txp_in[...].astype(F32)
    text_norm = raw_ref[...] * text_factor
    along = jnp.sum(text_norm * total, axis=1, keepdims=True)
    text_raw_grad = (text_factor * (total - text_norm * along)).astype(BF16)
    out_text[...] = dot_t(text_raw_grad, head[...])

    imp[0].wait_recv()
    out_loss[...] = loss_row + lossp_in[0:1, :]
    for half in range(2):
        imp[1 + half].wait_recv()
        top, end = half * HALF_ROWS, (half + 1) * HALF_ROWS
        factor = image_factor[top:end, :]
        total = sum_own[top:end, :] + imp_in[top:end, :].astype(F32)
        image_norm = images[top:end, :].astype(F32) * factor
        along = jnp.sum(image_norm * total, axis=1, keepdims=True)
        out_image[top:end, :] = factor * (total - image_norm * along)

    for copy in swap_a1 + swap_b1 + swap_a2 + swap_b2 + im_near + im_far + im_x + tx_near + tx_far + tx_x:
        copy.wait_send()
    for copy in [txp] + imp:
        copy.wait_send()


def settle(image_in, text_in, loss_in, image_out, text_out, loss_out, sem):
    copies = [
        pltpu.make_async_copy(src, dst, sem.at[i])
        for i, (src, dst) in enumerate(((image_in, image_out), (text_in, text_out), (loss_in, loss_out)))
    ]
    for copy in copies:
        copy.start()
    for copy in copies:
        copy.wait()


def per_device(
    tokens, lengths, caption_ids, destination, slot, images, image_ids, head_weight, logit_scale, logit_bias
):
    any_spec = pl.BlockSpec(memory_space=pl.ANY)
    vmem_spec = pl.BlockSpec(memory_space=pltpu.VMEM)
    smem_spec = pl.BlockSpec(memory_space=pltpu.SMEM)

    def vmem(shape, dtype):
        return pltpu.VMEM(shape, dtype)

    block = (ROWS, D)
    flat_tokens = jnp.transpose(tokens, (1, 0, 2)).reshape(TOKENS * CAPS_HERE, D)
    as_row = lambda a: a.reshape(1, a.shape[0])
    image_grad, text_grad, loss = pl.pallas_call(
        kernel,
        out_shape=(pltpu.VMEM(block, F32), pltpu.VMEM(block, F32), pltpu.VMEM((1, ROWS), F32)),
        in_specs=[any_spec] * 8 + [smem_spec] * 2,
        out_specs=(vmem_spec,) * 3,
        scratch_shapes=[
            vmem((TOKENS * CAPS_HERE, D), BF16),
            vmem((4, 1, CAPS_HERE), jnp.int32),
            vmem(block, BF16),
            vmem((1, ROWS), jnp.int32),
            vmem((D, D), BF16),
            vmem((5 * ROWS, D), BF16),
            vmem((5, 8, ROWS), F32),
            vmem(block, BF16),
            vmem((8, ROWS), F32),
            vmem((5 * ROWS, D), BF16),
            vmem((5, 8, ROWS), F32),
            vmem(block, BF16),
            vmem((8, ROWS), F32),
        ]
        + [vmem((ROWS, HALF), BF16)] * 8
        + [
            vmem(block, F32),
            vmem(block, F32),
            vmem(block, F32),
            vmem(block, F32),
            vmem(block, BF16),
            vmem(block, BF16),
            vmem(block, BF16),
            vmem(block, BF16),
            vmem((8, ROWS), F32),
            vmem((8, ROWS), F32),
            pltpu.SemaphoreType.DMA((8,)),
            pltpu.SemaphoreType.DMA((4, FAN)),
            pltpu.SemaphoreType.DMA((4, FAN)),
            pltpu.SemaphoreType.DMA((2, 5, PIECES)),
            pltpu.SemaphoreType.DMA((2, 5, PIECES)),
            pltpu.SemaphoreType.DMA((2, 5)),
            pltpu.SemaphoreType.DMA((2, 5)),
            pltpu.SemaphoreType.DMA((9,)),
            pltpu.SemaphoreType.DMA((9,)),
        ],
        compiler_params=pltpu.CompilerParams(
            collective_id=0, has_side_effects=True, vmem_limit_bytes=40 * 1024 * 1024
        ),
        name="band",
    )(
        *[
            pltpu.with_memory_space_constraint(a, pltpu.HBM)
            for a in (
                flat_tokens,
                as_row(lengths),
                as_row(caption_ids),
                as_row(destination),
                as_row(slot),
                images,
                as_row(image_ids),
                head_weight,
            )
        ],
        logit_scale,
        logit_bias,
    )
    image_grad, text_grad, loss = pl.pallas_call(
        settle,
        out_shape=(
            jax.ShapeDtypeStruct(block, F32),
            jax.ShapeDtypeStruct(block, F32),
            jax.ShapeDtypeStruct((1, ROWS), F32),
        ),
        in_specs=[vmem_spec] * 3,
        out_specs=(any_spec, any_spec, any_spec),
        scratch_shapes=[pltpu.SemaphoreType.DMA((3,))],
        compiler_params=pltpu.CompilerParams(vmem_limit_bytes=40 * 1024 * 1024),
        name="settle",
    )(image_grad, text_grad, loss)
    return (image_grad, text_grad, loss.reshape(ROWS))


def solution(mesh):
    spec1 = P(("blk", "group"))
    spec2 = P(("blk", "group"), None)
    return jax.shard_map(
        per_device,
        mesh=mesh,
        in_specs=(
            P(("blk", "group"), None, None),
            spec1,
            spec1,
            spec1,
            spec1,
            spec2,
            spec1,
            P(None, None),
            P(None),
            P(None),
        ),
        out_specs=(spec2, spec2, spec1),
        check_vma=False,
    )
```

```python
import jax
import jax.numpy as jnp
from jax import lax
from jax.experimental import pallas as pl
from jax.experimental.pallas import tpu as pltpu
from jax.sharding import PartitionSpec as P

D = 1152
ROWS = 128
CAPS_HERE = 48
TOKENS = 6
NORM_EPS = 1e-06
HALF = 640
FAN = 8
PIECES = 2
PIECE = ROWS // PIECES
PEER, CROSS, FAR = 5, 5, 8
FAR_FIRST = (4, 3, 5, 2, 6, 1, 7)
MESH = pl.DeviceIdType.MESH
BF16 = jnp.bfloat16
F32 = jnp.float32


def iota(shape, dim):
    return lax.broadcasted_iota(jnp.int32, shape, dim)


def dot(a, b):
    return lax.dot_general(a, b, (((1,), (0,)), ((), ())), preferred_element_type=F32)


def dot_t(a, b):
    return lax.dot_general(a, b, (((1,), (1,)), ((), ())), preferred_element_type=F32)


def swap_pairs(r):
    return ((r >> 1) & 7) * 16 + (r >> 4) * 2 + (r & 1)


def kernel(
    tokens_hbm,
    lengths_hbm,
    caption_ids_hbm,
    destination_hbm,
    slot_hbm,
    images_hbm,
    image_ids_hbm,
    head_hbm,
    scale_ref,
    bias_ref,
    out_image,
    out_text,
    out_loss,
    tokens,
    meta,
    images,
    image_ids_in,
    head,
    im_buf,
    im_ids,
    tx_buf,
    tx_ids,
    send_a1,
    recv_a1,
    send_a2,
    recv_a2,
    send_b1,
    recv_b1,
    send_b2,
    recv_b2,
    raw_ref,
    image_sum,
    text_sum,
    txp_out,
    txp_in,
    in_sem,
    swap_send,
    swap_recv,
    z_send,
    z_recv,
    zid_send,
    zid_recv,
    x_send,
    x_recv,
):
    blk = lax.axis_index("blk")
    grp = lax.axis_index("group")
    col = blk % 2
    peer = {"blk": blk + 1 - 2 * col}
    up = {"blk": (blk + 2) % 16}
    down = {"blk": (blk + 14) % 16}
    y, u = grp // FAN, grp % FAN
    y_peer = [{"group": ((y + k) % FAN) * FAN + u} for k in range(FAN)]
    u_peer = [{"group": y * FAN + (u + k) % FAN} for k in range(FAN)]

    loads = [
        pltpu.make_async_copy(src, dst, in_sem.at[i])
        for i, (src, dst) in enumerate(
            [
                (lengths_hbm, meta.at[0]),
                (destination_hbm, meta.at[1]),
                (slot_hbm, meta.at[2]),
                (caption_ids_hbm, meta.at[3]),
                (tokens_hbm, tokens),
                (images_hbm, images),
                (image_ids_hbm, image_ids_in),
                (head_hbm, head),
            ]
        )
    ]
    for load in loads[:5]:
        load.start()

    barrier = pltpu.get_barrier_semaphore()
    greeted = [peer, up, down] + y_peer[1:] + u_peer[1:]
    for other in greeted:
        pl.semaphore_signal(barrier, inc=1, device_id=other, device_id_type=MESH)
    for load in loads[5:7]:
        load.start()

    def remote(src, dst, send, recv, to):
        return pltpu.make_async_remote_copy(
            src_ref=src, dst_ref=dst, send_sem=send, recv_sem=recv, device_id=to, device_id_type=MESH
        )

    for i in range(4):
        loads[i].wait()
    lengths = meta[0]
    position = meta[1] * 2 + meta[2]
    places = 288
    spread = iota((CAPS_HERE, places), 1) - iota((CAPS_HERE, places), 0)
    hit = spread == 0
    level = jnp.zeros((1, places), jnp.int32)
    lane = iota((1, places), 1)
    for step in range(1, TOKENS):
        hit = hit | (spread == CAPS_HERE * step)
        level = level + (lane >= CAPS_HERE * step).astype(jnp.int32)
    spread_b = hit.astype(F32).astype(BF16)
    wide_length = dot(jnp.broadcast_to(lengths, (16, CAPS_HERE)).astype(F32).astype(BF16), spread_b)[0:1, :]
    wide_position = dot(jnp.broadcast_to(position, (16, CAPS_HERE)).astype(F32).astype(BF16), spread_b)[0:1, :]
    wide_position = jnp.where(level.astype(F32) < wide_length, wide_position, -1.0)

    def row_slot(r):
        return ((y + (r >> 4)) % FAN) * 16 + ((u + ((r >> 1) & 7)) % FAN) * 2 + (r & 1)

    def gather_matrix(order):
        return (order.astype(F32) == wide_position).astype(F32).astype(BF16)

    def own_captions(order):
        return order == position

    loads[4].wait()
    loads[7].start()
    order_a = row_slot(iota((ROWS, 1), 0))
    order_b = row_slot(swap_pairs(iota((ROWS, 1), 0)))
    here_a = own_captions(order_a)
    here_b = own_captions(order_b)
    count_a = jnp.sum(jnp.where(here_a, lengths, 0).astype(F32), axis=1, keepdims=True)
    count_b = jnp.sum(jnp.where(here_b, lengths, 0).astype(F32), axis=1, keepdims=True)
    ids_b = jnp.sum(jnp.where(here_b, meta[3] + 1, 0).astype(F32), axis=1, keepdims=True).astype(jnp.int32)
    send_a1[...] = (dot(gather_matrix(order_a), tokens[:, 0:HALF]) / jnp.maximum(count_a, 1.0)).astype(BF16)
    send_b1[:, 0 : D - HALF] = (
        dot(gather_matrix(order_b), tokens[:, HALF:D]) / jnp.maximum(count_b, 1.0)
    ).astype(BF16)
    id_lane = iota((ROWS, ROWS), 1)
    send_b1[:, D - HALF : HALF] = (
        jnp.where(id_lane == 0, ids_b >> 5, jnp.where(id_lane == 1, ids_b & 31, 0)).astype(F32).astype(BF16)
    )

    pl.semaphore_wait(barrier, len(greeted))

    def swap(stages):
        copies = [[] for _ in stages]
        for k in FAR_FIRST:
            for i, (stage, src, dst, to) in enumerate(stages):
                copy = remote(
                    src.at[pl.ds(k * 16, 16)],
                    dst.at[pl.ds(k * 16, 16)],
                    swap_send.at[stage, k],
                    swap_recv.at[stage, k],
                    to[k],
                )
                copy.start()
                copies[i].append(copy)
        for stage, src, dst, to in stages:
            dst[0:16, :] = src[0:16, :]
        return copies

    ways = ((up, 1), (down, 2))

    def start_piece(kind, buf, piece, start=0, land=0):
        copies = []
        for to, place in ways:
            copy = remote(
                buf.at[pl.ds(start * ROWS + piece * PIECE, PIECE)],
                buf.at[pl.ds((land + place) * ROWS + piece * PIECE, PIECE)],
                z_send.at[kind, place, piece],
                z_recv.at[kind, place, piece],
                to,
            )
            copy.start()
            copies.append(copy)
        return copies

    def start_ids(kind, ids, start=0, land=0):
        copies = []
        for to, place in ways:
            copy = remote(
                ids.at[start], ids.at[land + place], zid_send.at[kind, place], zid_recv.at[kind, place], to
            )
            copy.start()
            copies.append(copy)
        return copies

    def own_along_z(kind, buf, ids):
        copies = []
        for piece in range(PIECES):
            copies += start_piece(kind, buf, piece)
        return copies + start_ids(kind, ids)

    def pass_piece(kind, buf, arriving, piece):
        copies = []
        for way, (to, place) in enumerate(ways):
            arriving[piece * 2 + way].wait_recv()
            far = place + 2
            copy = remote(
                buf.at[pl.ds(place * ROWS + piece * PIECE, PIECE)],
                buf.at[pl.ds(far * ROWS + piece * PIECE, PIECE)],
                z_send.at[kind, far, piece],
                z_recv.at[kind, far, piece],
                to,
            )
            copy.start()
            copies.append(copy)
        return copies

    def pass_ids(kind, ids, arriving):
        copies = []
        for way, (to, place) in enumerate(ways):
            arriving[PIECES * 2 + way].wait_recv()
            far = place + 2
            copy = remote(ids.at[place], ids.at[far], zid_send.at[kind, far], zid_recv.at[kind, far], to)
            copy.start()
            copies.append(copy)
        return copies

    def to_peer(i, src, dst):
        copy = remote(src, dst, x_send.at[i], x_recv.at[i], peer)
        copy.start()
        return copy

    swap_a1, swap_b1 = swap([(0, send_a1, recv_a1, y_peer), (1, send_b1, recv_b1, u_peer)])

    loads[5].wait()
    loads[6].wait()
    image_f = images[...].astype(F32)
    image_factor = lax.rsqrt(jnp.sum(image_f * image_f, axis=1, keepdims=True) + NORM_EPS)
    im_buf[0:ROWS, :] = (image_f * image_factor).astype(BF16)
    im_ids[0] = jnp.broadcast_to(image_ids_in[...].astype(F32), (8, ROWS))
    im_near = own_along_z(0, im_buf, im_ids)

    r_out = iota((ROWS, ROWS), 0)
    r_in = iota((ROWS, ROWS), 1)
    turn = (swap_pairs(r_out) == r_in).astype(F32).astype(BF16)
    for copy in swap_a1:
        copy.wait_recv()
    send_a2[...] = dot(turn, recv_a1[...]).astype(BF16)
    (swap_a2,) = swap([(2, send_a2, recv_a2, u_peer)])
    for copy in swap_b1:
        copy.wait_recv()
    send_b2[...] = dot(turn, recv_b1[...]).astype(BF16)
    (swap_b2,) = swap([(3, send_b2, recv_b2, y_peer)])

    im_far = []
    for piece in range(PIECES):
        im_far += pass_piece(0, im_buf, im_near, piece)
    im_far += pass_ids(0, im_ids, im_near)

    def home_slot(r):
        return ((y + FAN - (r >> 4)) % FAN) * 16 + ((u + FAN - ((r >> 1) & 7)) % FAN) * 2 + (r & 1)

    home_a = (home_slot(swap_pairs(r_in)) == r_out).astype(F32).astype(BF16)
    home_b = (home_slot(r_in) == r_out).astype(F32).astype(BF16)
    for copy in swap_a2:
        copy.wait_recv()
    pooled_a = dot(home_a, recv_a2[...]).astype(BF16)
    loads[7].wait()
    raw_a = dot(pooled_a, head[0:HALF, :])
    for copy in swap_b2:
        copy.wait_recv()
    pooled_b = dot(home_b, recv_b2[...]).astype(BF16)
    raw = raw_a + dot(pooled_b[:, 0 : D - HALF], head[HALF:D, :])
    text_factor = lax.rsqrt(jnp.sum(raw * raw, axis=1, keepdims=True) + NORM_EPS)
    tx_near, tx_x = [], []
    for piece in range(PIECES):
        rows = pl.ds(piece * PIECE, PIECE)
        top, end = piece * PIECE, (piece + 1) * PIECE
        tx_buf[rows, :] = (raw[top:end, :] * text_factor[top:end, :]).astype(BF16)
        tx_near += start_piece(1, tx_buf, piece)
        tx_x.append(to_peer(piece, tx_buf.at[rows], tx_buf.at[pl.ds(PEER * ROWS + piece * PIECE, PIECE)]))
    id_codes = pooled_b[:, D - HALF : HALF]
    weigh_in = jnp.where(r_in == 0, 32.0, jnp.where(r_in == 1, 1.0, 0.0)).astype(BF16)
    tx_cols = dot_t(weigh_in, id_codes) - 1.0
    tx_ids[0] = tx_cols[0:8, :]
    tx_near += start_ids(1, tx_ids)
    tx_x.append(to_peer(2, tx_ids.at[0], tx_ids.at[PEER]))
    raw_ref[...] = raw

    scale = scale_ref[0]
    bias = bias_ref[0]

    def as_rows(ids):
        return jnp.transpose(jnp.broadcast_to(ids, (ROWS, ROWS)))

    def terms(rows, row_ids, cols, col_ids, text_is_rows, far_masks):
        logits = scale * dot_t(rows, cols) + bias
        blocks = len(col_ids)
        wide_cols = jnp.concatenate(col_ids, axis=1)
        wide_rows = jnp.concatenate([row_ids] * blocks, axis=1)
        same = wide_rows == wide_cols
        live = ((wide_rows if text_is_rows else wide_cols) >= 0.0).astype(F32)
        if far_masks is not None:
            ones = jnp.ones((1, ROWS), F32)
            allowed = jnp.concatenate(
                [ones] * (blocks - 2) + [ones * far_masks[0], ones * far_masks[1]], axis=1
            )
            live = live * allowed
        flipped = jnp.where(same, -logits, logits)
        small = jnp.exp(-jnp.abs(flipped))
        sigmoid = jnp.where(flipped >= 0.0, 1.0, small) / (1.0 + small)
        weights = (live * jnp.where(same, -scale, scale) * sigmoid).astype(BF16)
        if text_is_rows:
            return weights, None
        softplus = jnp.maximum(flipped, 0.0) + jnp.log1p(small)
        return weights, jnp.sum(live * softplus, axis=1, keepdims=True)

    col_f = col.astype(F32)
    far_masks = (col_f, 1.0 - col_f)

    for copy in im_far:
        copy.wait_recv()
    im_cols = [im_ids[place][0:1, :] for place in range(5)]
    weights, _ = terms(tx_buf[0:ROWS, :], as_rows(tx_cols[0:1, :]), im_buf[...], im_cols, True, None)
    text_sum[...] = dot(weights, im_buf[...])
    im_rows = as_rows(im_ids[0][0:1, :])

    tx_far, tx_cross, txp = [], [], []
    for piece in range(PIECES):
        tx_far += pass_piece(1, tx_buf, tx_near, piece)
        tx_x[piece].wait_recv()
        if piece == 0:
            tx_x[PIECES].wait_recv()
            peer_rows = as_rows(tx_ids[PEER][0:1, :])
        if piece == PIECES - 1:
            tx_far += pass_ids(1, tx_ids, tx_near)
            for part in range(PIECES):
                tx_cross += start_piece(2, tx_buf, part, PEER, CROSS)
            tx_cross += start_ids(2, tx_ids, PEER, CROSS)
        top, end = piece * PIECE, (piece + 1) * PIECE
        peer_text = tx_buf[PEER * ROWS + top : PEER * ROWS + end, :]
        weights, _ = terms(peer_text, peer_rows[top:end, :], im_buf[...], im_cols, True, far_masks)
        txp_out[top:end, :] = dot(weights, im_buf[...]).astype(BF16)
        txp.append(to_peer(3 + piece, txp_out.at[pl.ds(top, PIECE)], txp_in.at[pl.ds(top, PIECE)]))

    def image_terms(place, blocks):
        cols = tx_buf[place * ROWS : (place + blocks) * ROWS, :]
        ids = [tx_ids[p][0:1, :] for p in range(place, place + blocks)]
        weights, loss = terms(im_buf[0:ROWS, :], im_rows, cols, ids, False, None)
        return dot(weights, cols), loss

    part, loss_own = image_terms(0, 3)
    image_sum[...] = part
    part, loss = image_terms(PEER, 1)
    image_sum[...] += part
    loss_own = loss_own + loss

    lacking = 4 - col
    tx_last = []
    for piece in range(PIECES):
        for way in range(2):
            tx_far[piece * 2 + way].wait_recv()
        tx_last.append(
            to_peer(
                5 + piece,
                tx_buf.at[pl.ds(pl.multiple_of(lacking * ROWS + piece * PIECE, PIECE), PIECE)],
                tx_buf.at[pl.ds(FAR * ROWS + piece * PIECE, PIECE)],
            )
        )
    for way in range(2):
        tx_far[PIECES * 2 + way].wait_recv()
    tx_last.append(to_peer(7, tx_ids.at[lacking], tx_ids.at[FAR]))
    part, loss = image_terms(3, 2)
    image_sum[...] += part
    loss_own = loss_own + loss

    for copy in txp:
        copy.wait_recv()
    total = text_sum[...] + txp_in[...].astype(F32)
    text_norm = raw_ref[...] * text_factor
    along = jnp.sum(text_norm * total, axis=1, keepdims=True)
    text_raw_grad = (text_factor * (total - text_norm * along)).astype(BF16)
    out_text[...] = dot_t(text_raw_grad, head[...])

    for copy in tx_cross + tx_last:
        copy.wait_recv()
    part, loss = image_terms(CROSS + 1, 3)
    loss_own = loss_own + loss
    total = image_sum[...] + part
    image_norm = images[...].astype(F32) * image_factor
    along = jnp.sum(image_norm * total, axis=1, keepdims=True)
    out_image[...] = image_factor * (total - image_norm * along)
    out_loss[...] = jnp.transpose(jnp.broadcast_to(loss_own, (ROWS, ROWS)))[0:1, :]

    for copy in swap_a1 + swap_b1 + swap_a2 + swap_b2 + im_near + im_far:
        copy.wait_send()
    for copy in tx_near + tx_far + tx_x + tx_cross + txp + tx_last:
        copy.wait_send()


def settle(image_in, text_in, loss_in, image_out, text_out, loss_out, sem):
    copies = [
        pltpu.make_async_copy(src, dst, sem.at[i])
        for i, (src, dst) in enumerate(((image_in, image_out), (text_in, text_out), (loss_in, loss_out)))
    ]
    for copy in copies:
        copy.start()
    for copy in copies:
        copy.wait()


def per_device(
    tokens, lengths, caption_ids, destination, slot, images, image_ids, head_weight, logit_scale, logit_bias
):
    any_spec = pl.BlockSpec(memory_space=pl.ANY)
    vmem_spec = pl.BlockSpec(memory_space=pltpu.VMEM)
    smem_spec = pl.BlockSpec(memory_space=pltpu.SMEM)

    def vmem(shape, dtype):
        return pltpu.VMEM(shape, dtype)

    block = (ROWS, D)
    flat_tokens = jnp.transpose(tokens, (1, 0, 2)).reshape(TOKENS * CAPS_HERE, D)
    as_row = lambda a: a.reshape(1, a.shape[0])
    image_grad, text_grad, loss = pl.pallas_call(
        kernel,
        out_shape=(pltpu.VMEM(block, F32), pltpu.VMEM(block, F32), pltpu.VMEM((1, ROWS), F32)),
        in_specs=[any_spec] * 8 + [smem_spec] * 2,
        out_specs=(vmem_spec,) * 3,
        scratch_shapes=[
            vmem((TOKENS * CAPS_HERE, D), BF16),
            vmem((4, 1, CAPS_HERE), jnp.int32),
            vmem(block, BF16),
            vmem((1, ROWS), jnp.int32),
            vmem((D, D), BF16),
            vmem((5 * ROWS, D), BF16),
            vmem((5, 8, ROWS), F32),
            vmem((9 * ROWS, D), BF16),
            vmem((9, 8, ROWS), F32),
        ]
        + [vmem((ROWS, HALF), BF16)] * 8
        + [
            vmem(block, F32),
            vmem(block, F32),
            vmem(block, F32),
            vmem(block, BF16),
            vmem(block, BF16),
            pltpu.SemaphoreType.DMA((8,)),
            pltpu.SemaphoreType.DMA((4, FAN)),
            pltpu.SemaphoreType.DMA((4, FAN)),
            pltpu.SemaphoreType.DMA((3, 5, PIECES)),
            pltpu.SemaphoreType.DMA((3, 5, PIECES)),
            pltpu.SemaphoreType.DMA((3, 5)),
            pltpu.SemaphoreType.DMA((3, 5)),
            pltpu.SemaphoreType.DMA((8,)),
            pltpu.SemaphoreType.DMA((8,)),
        ],
        compiler_params=pltpu.CompilerParams(
            collective_id=0, has_side_effects=True, vmem_limit_bytes=40 * 1024 * 1024
        ),
        name="band",
    )(
        *[
            pltpu.with_memory_space_constraint(a, pltpu.HBM)
            for a in (
                flat_tokens,
                as_row(lengths),
                as_row(caption_ids),
                as_row(destination),
                as_row(slot),
                images,
                as_row(image_ids),
                head_weight,
            )
        ],
        logit_scale,
        logit_bias,
    )
    image_grad, text_grad, loss = pl.pallas_call(
        settle,
        out_shape=(
            jax.ShapeDtypeStruct(block, F32),
            jax.ShapeDtypeStruct(block, F32),
            jax.ShapeDtypeStruct((1, ROWS), F32),
        ),
        in_specs=[vmem_spec] * 3,
        out_specs=(any_spec, any_spec, any_spec),
        scratch_shapes=[pltpu.SemaphoreType.DMA((3,))],
        compiler_params=pltpu.CompilerParams(vmem_limit_bytes=40 * 1024 * 1024),
        name="settle",
    )(image_grad, text_grad, loss)
    return (image_grad, text_grad, loss.reshape(ROWS))


def solution(mesh):
    spec1 = P(("blk", "group"))
    spec2 = P(("blk", "group"), None)
    return jax.shard_map(
        per_device,
        mesh=mesh,
        in_specs=(
            P(("blk", "group"), None, None),
            spec1,
            spec1,
            spec1,
            spec1,
            spec2,
            spec1,
            P(None, None),
            P(None),
            P(None),
        ),
        out_specs=(spec2, spec2, spec1),
        check_vma=False,
    )
```

```python
import jax
import jax.numpy as jnp
from jax import lax
from jax.experimental import pallas as pl
from jax.experimental.pallas import tpu as pltpu
from jax.sharding import PartitionSpec as P

D = 1152
ROWS = 128
CAPS_HERE = 48
TOKENS = 6
NORM_EPS = 1e-06
HALF = 640
FAN = 8
PIECES = 2
PIECE = ROWS // PIECES
PEER, CROSS, FAR = 5, 5, 8
FAR_FIRST = (4, 3, 5, 2, 6, 1, 7)
MESH = pl.DeviceIdType.MESH
BF16 = jnp.bfloat16
F32 = jnp.float32


def iota(shape, dim):
    return lax.broadcasted_iota(jnp.int32, shape, dim)


def dot(a, b):
    return lax.dot_general(a, b, (((1,), (0,)), ((), ())), preferred_element_type=F32)


def dot_t(a, b):
    return lax.dot_general(a, b, (((1,), (1,)), ((), ())), preferred_element_type=F32)


def swap_pairs(r):
    return ((r >> 1) & 7) * 16 + (r >> 4) * 2 + (r & 1)


def kernel(
    tokens_hbm,
    lengths_hbm,
    caption_ids_hbm,
    destination_hbm,
    slot_hbm,
    images_hbm,
    image_ids_hbm,
    head_hbm,
    scale_ref,
    bias_ref,
    out_image,
    out_text,
    out_loss,
    tokens,
    meta,
    images,
    image_ids_in,
    head,
    im_buf,
    im_ids,
    tx_buf,
    tx_ids,
    send_a1,
    recv_a1,
    send_a2,
    recv_a2,
    send_b1,
    recv_b1,
    send_b2,
    recv_b2,
    raw_ref,
    image_sum,
    text_sum,
    txp_out,
    txp_in,
    in_sem,
    swap_send,
    swap_recv,
    z_send,
    z_recv,
    zid_send,
    zid_recv,
    x_send,
    x_recv,
):
    blk = lax.axis_index("blk")
    grp = lax.axis_index("group")
    col = blk % 2
    peer = {"blk": blk + 1 - 2 * col}
    up = {"blk": (blk + 2) % 16}
    down = {"blk": (blk + 14) % 16}
    y, u = grp // FAN, grp % FAN
    y_peer = [{"group": ((y + k) % FAN) * FAN + u} for k in range(FAN)]
    u_peer = [{"group": y * FAN + (u + k) % FAN} for k in range(FAN)]

    loads = [
        pltpu.make_async_copy(src, dst, in_sem.at[i])
        for i, (src, dst) in enumerate(
            [
                (lengths_hbm, meta.at[0]),
                (destination_hbm, meta.at[1]),
                (slot_hbm, meta.at[2]),
                (caption_ids_hbm, meta.at[3]),
                (tokens_hbm, tokens),
                (images_hbm, images),
                (image_ids_hbm, image_ids_in),
                (head_hbm, head),
            ]
        )
    ]
    for load in loads[:5]:
        load.start()

    barrier = pltpu.get_barrier_semaphore()
    greeted = [peer, up, down] + y_peer[1:] + u_peer[1:]
    for other in greeted:
        pl.semaphore_signal(barrier, inc=1, device_id=other, device_id_type=MESH)
    for load in loads[5:7]:
        load.start()

    def remote(src, dst, send, recv, to):
        return pltpu.make_async_remote_copy(
            src_ref=src, dst_ref=dst, send_sem=send, recv_sem=recv, device_id=to, device_id_type=MESH
        )

    for i in range(4):
        loads[i].wait()
    lengths = meta[0]
    position = meta[1] * 2 + meta[2]
    places = 288
    spread = iota((CAPS_HERE, places), 1) - iota((CAPS_HERE, places), 0)
    hit = spread == 0
    level = jnp.zeros((1, places), jnp.int32)
    lane = iota((1, places), 1)
    for step in range(1, TOKENS):
        hit = hit | (spread == CAPS_HERE * step)
        level = level + (lane >= CAPS_HERE * step).astype(jnp.int32)
    spread_b = hit.astype(F32).astype(BF16)
    wide_length = dot(jnp.broadcast_to(lengths, (16, CAPS_HERE)).astype(F32).astype(BF16), spread_b)[0:1, :]
    wide_position = dot(jnp.broadcast_to(position, (16, CAPS_HERE)).astype(F32).astype(BF16), spread_b)[0:1, :]
    wide_position = jnp.where(level.astype(F32) < wide_length, wide_position, -1.0)

    def row_slot(r):
        return ((y + (r >> 4)) % FAN) * 16 + ((u + ((r >> 1) & 7)) % FAN) * 2 + (r & 1)

    def gather_matrix(order):
        return (order.astype(F32) == wide_position).astype(F32).astype(BF16)

    def own_captions(order):
        return order == position

    loads[4].wait()
    loads[7].start()
    order_a = row_slot(iota((ROWS, 1), 0))
    order_b = row_slot(swap_pairs(iota((ROWS, 1), 0)))
    here_a = own_captions(order_a)
    here_b = own_captions(order_b)
    count_a = jnp.sum(jnp.where(here_a, lengths, 0).astype(F32), axis=1, keepdims=True)
    count_b = jnp.sum(jnp.where(here_b, lengths, 0).astype(F32), axis=1, keepdims=True)
    ids_b = jnp.sum(jnp.where(here_b, meta[3] + 1, 0).astype(F32), axis=1, keepdims=True).astype(jnp.int32)
    send_a1[...] = (dot(gather_matrix(order_a), tokens[:, 0:HALF]) / jnp.maximum(count_a, 1.0)).astype(BF16)
    send_b1[:, 0 : D - HALF] = (
        dot(gather_matrix(order_b), tokens[:, HALF:D]) / jnp.maximum(count_b, 1.0)
    ).astype(BF16)
    id_lane = iota((ROWS, ROWS), 1)
    send_b1[:, D - HALF : HALF] = (
        jnp.where(id_lane == 0, ids_b >> 5, jnp.where(id_lane == 1, ids_b & 31, 0)).astype(F32).astype(BF16)
    )

    pl.semaphore_wait(barrier, len(greeted))

    def swap(stages):
        for k in FAR_FIRST:
            for stage, src, dst, to in stages:
                rows = pl.ds(k * 16, 16)
                remote(src.at[rows], dst.at[rows], swap_send.at[stage], swap_recv.at[stage], to[k]).start()
        alls = []
        for stage, src, dst, to in stages:
            dst[0:16, :] = src[0:16, :]
            rows = pl.ds(16, ROWS - 16)
            alls.append([remote(src.at[rows], dst.at[rows], swap_send.at[stage], swap_recv.at[stage], to[1])])
        return alls

    ways = ((up, 1), (down, 2))

    def start_piece(kind, buf, piece, start=0, land=0):
        copies = []
        for to, place in ways:
            copy = remote(
                buf.at[pl.ds(start * ROWS + piece * PIECE, PIECE)],
                buf.at[pl.ds((land + place) * ROWS + piece * PIECE, PIECE)],
                z_send.at[kind, place, piece],
                z_recv.at[kind, place, piece],
                to,
            )
            copy.start()
            copies.append(copy)
        return copies

    def start_ids(kind, ids, start=0, land=0):
        copies = []
        for to, place in ways:
            copy = remote(
                ids.at[start], ids.at[land + place], zid_send.at[kind, place], zid_recv.at[kind, place], to
            )
            copy.start()
            copies.append(copy)
        return copies

    def own_along_z(kind, buf, ids):
        copies = []
        for piece in range(PIECES):
            copies += start_piece(kind, buf, piece)
        return copies + start_ids(kind, ids)

    def pass_piece(kind, buf, arriving, piece):
        copies = []
        for way, (to, place) in enumerate(ways):
            arriving[piece * 2 + way].wait_recv()
            far = place + 2
            copy = remote(
                buf.at[pl.ds(place * ROWS + piece * PIECE, PIECE)],
                buf.at[pl.ds(far * ROWS + piece * PIECE, PIECE)],
                z_send.at[kind, far, piece],
                z_recv.at[kind, far, piece],
                to,
            )
            copy.start()
            copies.append(copy)
        return copies

    def pass_ids(kind, ids, arriving):
        copies = []
        for way, (to, place) in enumerate(ways):
            arriving[PIECES * 2 + way].wait_recv()
            far = place + 2
            copy = remote(ids.at[place], ids.at[far], zid_send.at[kind, far], zid_recv.at[kind, far], to)
            copy.start()
            copies.append(copy)
        return copies

    def to_peer(i, src, dst):
        copy = remote(src, dst, x_send.at[i], x_recv.at[i], peer)
        copy.start()
        return copy

    swap_a1, swap_b1 = swap([(0, send_a1, recv_a1, y_peer), (1, send_b1, recv_b1, u_peer)])

    loads[5].wait()
    loads[6].wait()
    image_f = images[...].astype(F32)
    image_factor = lax.rsqrt(jnp.sum(image_f * image_f, axis=1, keepdims=True) + NORM_EPS)
    im_buf[0:ROWS, :] = (image_f * image_factor).astype(BF16)
    im_ids[0] = jnp.broadcast_to(image_ids_in[...].astype(F32), (8, ROWS))
    im_near = own_along_z(0, im_buf, im_ids)

    r_out = iota((ROWS, ROWS), 0)
    r_in = iota((ROWS, ROWS), 1)
    turn = (swap_pairs(r_out) == r_in).astype(F32).astype(BF16)
    for copy in swap_a1:
        copy.wait_recv()
    send_a2[...] = dot(turn, recv_a1[...]).astype(BF16)
    (swap_a2,) = swap([(2, send_a2, recv_a2, u_peer)])
    for copy in swap_b1:
        copy.wait_recv()
    send_b2[...] = dot(turn, recv_b1[...]).astype(BF16)
    (swap_b2,) = swap([(3, send_b2, recv_b2, y_peer)])

    im_far = []
    for piece in range(PIECES):
        im_far += pass_piece(0, im_buf, im_near, piece)
    im_far += pass_ids(0, im_ids, im_near)

    def home_slot(r):
        return ((y + FAN - (r >> 4)) % FAN) * 16 + ((u + FAN - ((r >> 1) & 7)) % FAN) * 2 + (r & 1)

    home = (home_slot(r_in) == r_out).astype(F32).astype(BF16)
    for copy in swap_a2:
        copy.wait_recv()
    pooled_a = dot(turn, recv_a2[...]).astype(BF16)
    loads[7].wait()
    raw_a = dot(pooled_a, head[0:HALF, :])
    for copy in swap_b2:
        copy.wait_recv()
    raw = raw_a + dot(recv_b2[:, 0 : D - HALF], head[HALF:D, :])
    text_factor = lax.rsqrt(jnp.sum(raw * raw, axis=1, keepdims=True) + NORM_EPS)
    tx_near, tx_x = [], []
    for piece in range(PIECES):
        rows = pl.ds(piece * PIECE, PIECE)
        top, end = piece * PIECE, (piece + 1) * PIECE
        tx_buf[rows, :] = (raw[top:end, :] * text_factor[top:end, :]).astype(BF16)
        tx_near += start_piece(1, tx_buf, piece)
        tx_x.append(to_peer(piece, tx_buf.at[rows], tx_buf.at[pl.ds(PEER * ROWS + piece * PIECE, PIECE)]))
    id_codes = recv_b2[:, D - HALF : HALF]
    weigh_in = jnp.where(r_in == 0, 32.0, jnp.where(r_in == 1, 1.0, 0.0)).astype(BF16)
    tx_cols = dot_t(weigh_in, id_codes) - 1.0
    tx_ids[0] = tx_cols[0:8, :]
    tx_near += start_ids(1, tx_ids)
    tx_x.append(to_peer(2, tx_ids.at[0], tx_ids.at[PEER]))
    raw_ref[...] = raw

    scale = scale_ref[0]
    bias = bias_ref[0]

    def as_rows(ids):
        return jnp.transpose(jnp.broadcast_to(ids, (ROWS, ROWS)))

    def terms(rows, row_ids, cols, col_ids, text_is_rows, far_masks):
        logits = scale * dot_t(rows, cols) + bias
        blocks = len(col_ids)
        wide_cols = jnp.concatenate(col_ids, axis=1)
        wide_rows = jnp.concatenate([row_ids] * blocks, axis=1)
        same = wide_rows == wide_cols
        live = ((wide_rows if text_is_rows else wide_cols) >= 0.0).astype(F32)
        if far_masks is not None:
            ones = jnp.ones((1, ROWS), F32)
            allowed = jnp.concatenate(
                [ones] * (blocks - 2) + [ones * far_masks[0], ones * far_masks[1]], axis=1
            )
            live = live * allowed
        flipped = jnp.where(same, -logits, logits)
        small = jnp.exp(-jnp.abs(flipped))
        sigmoid = jnp.where(flipped >= 0.0, 1.0, small) / (1.0 + small)
        weights = (live * jnp.where(same, -scale, scale) * sigmoid).astype(BF16)
        if text_is_rows:
            return weights, None
        softplus = jnp.maximum(flipped, 0.0) + jnp.log1p(small)
        return weights, jnp.sum(live * softplus, axis=1, keepdims=True)

    col_f = col.astype(F32)
    far_masks = (col_f, 1.0 - col_f)

    for copy in im_far:
        copy.wait_recv()
    im_cols = [im_ids[place][0:1, :] for place in range(5)]
    weights, _ = terms(tx_buf[0:ROWS, :], as_rows(tx_cols[0:1, :]), im_buf[...], im_cols, True, None)
    text_sum[...] = dot(weights, im_buf[...])
    im_rows = as_rows(im_ids[0][0:1, :])

    tx_far, tx_cross, txp = [], [], []
    for piece in range(PIECES):
        tx_far += pass_piece(1, tx_buf, tx_near, piece)
        tx_x[piece].wait_recv()
        if piece == 0:
            tx_x[PIECES].wait_recv()
            peer_rows = as_rows(tx_ids[PEER][0:1, :])
        if piece == PIECES - 1:
            tx_far += pass_ids(1, tx_ids, tx_near)
            for part in range(PIECES):
                tx_cross += start_piece(2, tx_buf, part, PEER, CROSS)
            tx_cross += start_ids(2, tx_ids, PEER, CROSS)
        top, end = piece * PIECE, (piece + 1) * PIECE
        peer_text = tx_buf[PEER * ROWS + top : PEER * ROWS + end, :]
        weights, _ = terms(peer_text, peer_rows[top:end, :], im_buf[...], im_cols, True, far_masks)
        txp_out[top:end, :] = dot(weights, im_buf[...]).astype(BF16)
        txp.append(to_peer(3 + piece, txp_out.at[pl.ds(top, PIECE)], txp_in.at[pl.ds(top, PIECE)]))

    def image_terms(place, blocks):
        cols = tx_buf[place * ROWS : (place + blocks) * ROWS, :]
        ids = [tx_ids[p][0:1, :] for p in range(place, place + blocks)]
        weights, loss = terms(im_buf[0:ROWS, :], im_rows, cols, ids, False, None)
        return dot(weights, cols), loss

    part, loss_own = image_terms(0, 3)
    image_sum[...] = part
    part, loss = image_terms(PEER, 1)
    image_sum[...] += part
    loss_own = loss_own + loss

    lacking = 4 - col
    tx_last = []
    for piece in range(PIECES):
        for way in range(2):
            tx_far[piece * 2 + way].wait_recv()
        tx_last.append(
            to_peer(
                5 + piece,
                tx_buf.at[pl.ds(pl.multiple_of(lacking * ROWS + piece * PIECE, PIECE), PIECE)],
                tx_buf.at[pl.ds(FAR * ROWS + piece * PIECE, PIECE)],
            )
        )
    for way in range(2):
        tx_far[PIECES * 2 + way].wait_recv()
    tx_last.append(to_peer(7, tx_ids.at[lacking], tx_ids.at[FAR]))
    part, loss = image_terms(3, 2)
    image_sum[...] += part
    loss_own = loss_own + loss

    for copy in txp:
        copy.wait_recv()
    total = text_sum[...] + txp_in[...].astype(F32)
    text_norm = raw_ref[...] * text_factor
    along = jnp.sum(text_norm * total, axis=1, keepdims=True)
    text_raw_grad = (text_factor * (total - text_norm * along)).astype(BF16)
    out_text[...] = dot_t(dot(home, text_raw_grad).astype(BF16), head[...])

    for copy in swap_a1 + swap_b1 + swap_a2 + swap_b2 + im_near + im_far:
        copy.wait_send()
    for copy in tx_near + tx_x + txp + tx_far + tx_cross + tx_last:
        copy.wait_send()

    for copy in tx_cross + tx_last:
        copy.wait_recv()
    part, loss = image_terms(CROSS + 1, 3)
    loss_own = loss_own + loss
    total = image_sum[...] + part
    image_norm = images[...].astype(F32) * image_factor
    along = jnp.sum(image_norm * total, axis=1, keepdims=True)
    out_image[...] = image_factor * (total - image_norm * along)
    out_loss[...] = jnp.transpose(jnp.broadcast_to(loss_own, (ROWS, ROWS)))[0:1, :]


def settle(image_in, text_in, loss_in, image_out, text_out, loss_out, sem):
    copies = [
        pltpu.make_async_copy(src, dst, sem.at[i])
        for i, (src, dst) in enumerate(((image_in, image_out), (text_in, text_out), (loss_in, loss_out)))
    ]
    for copy in copies:
        copy.start()
    for copy in copies:
        copy.wait()


def per_device(
    tokens, lengths, caption_ids, destination, slot, images, image_ids, head_weight, logit_scale, logit_bias
):
    any_spec = pl.BlockSpec(memory_space=pl.ANY)
    vmem_spec = pl.BlockSpec(memory_space=pltpu.VMEM)
    smem_spec = pl.BlockSpec(memory_space=pltpu.SMEM)

    def vmem(shape, dtype):
        return pltpu.VMEM(shape, dtype)

    block = (ROWS, D)
    flat_tokens = jnp.transpose(tokens, (1, 0, 2)).reshape(TOKENS * CAPS_HERE, D)
    as_row = lambda a: a.reshape(1, a.shape[0])
    image_grad, text_grad, loss = pl.pallas_call(
        kernel,
        out_shape=(pltpu.VMEM(block, F32), pltpu.VMEM(block, F32), pltpu.VMEM((1, ROWS), F32)),
        in_specs=[any_spec] * 8 + [smem_spec] * 2,
        out_specs=(vmem_spec,) * 3,
        scratch_shapes=[
            vmem((TOKENS * CAPS_HERE, D), BF16),
            vmem((4, 1, CAPS_HERE), jnp.int32),
            vmem(block, BF16),
            vmem((1, ROWS), jnp.int32),
            vmem((D, D), BF16),
            vmem((5 * ROWS, D), BF16),
            vmem((5, 8, ROWS), F32),
            vmem((9 * ROWS, D), BF16),
            vmem((9, 8, ROWS), F32),
        ]
        + [vmem((ROWS, HALF), BF16)] * 8
        + [
            vmem(block, F32),
            vmem(block, F32),
            vmem(block, F32),
            vmem(block, BF16),
            vmem(block, BF16),
            pltpu.SemaphoreType.DMA((8,)),
            pltpu.SemaphoreType.DMA((4,)),
            pltpu.SemaphoreType.DMA((4,)),
            pltpu.SemaphoreType.DMA((3, 5, PIECES)),
            pltpu.SemaphoreType.DMA((3, 5, PIECES)),
            pltpu.SemaphoreType.DMA((3, 5)),
            pltpu.SemaphoreType.DMA((3, 5)),
            pltpu.SemaphoreType.DMA((8,)),
            pltpu.SemaphoreType.DMA((8,)),
        ],
        compiler_params=pltpu.CompilerParams(
            collective_id=0, has_side_effects=True, vmem_limit_bytes=40 * 1024 * 1024
        ),
        name="band",
    )(
        *[
            pltpu.with_memory_space_constraint(a, pltpu.HBM)
            for a in (
                flat_tokens,
                as_row(lengths),
                as_row(caption_ids),
                as_row(destination),
                as_row(slot),
                images,
                as_row(image_ids),
                head_weight,
            )
        ],
        logit_scale,
        logit_bias,
    )
    image_grad, text_grad, loss = pl.pallas_call(
        settle,
        out_shape=(
            jax.ShapeDtypeStruct(block, F32),
            jax.ShapeDtypeStruct(block, F32),
            jax.ShapeDtypeStruct((1, ROWS), F32),
        ),
        in_specs=[vmem_spec] * 3,
        out_specs=(any_spec, any_spec, any_spec),
        scratch_shapes=[pltpu.SemaphoreType.DMA((3,))],
        compiler_params=pltpu.CompilerParams(vmem_limit_bytes=40 * 1024 * 1024),
        name="settle",
    )(image_grad, text_grad, loss)
    return (image_grad, text_grad, loss.reshape(ROWS))


def solution(mesh):
    spec1 = P(("blk", "group"))
    spec2 = P(("blk", "group"), None)
    return jax.shard_map(
        per_device,
        mesh=mesh,
        in_specs=(
            P(("blk", "group"), None, None),
            spec1,
            spec1,
            spec1,
            spec1,
            spec2,
            spec1,
            P(None, None),
            P(None),
            P(None),
        ),
        out_specs=(spec2, spec2, spec1),
        check_vma=False,
    )
```

```python
import jax
import jax.numpy as jnp
from jax import lax
from jax.experimental import pallas as pl
from jax.experimental.pallas import tpu as pltpu
from jax.sharding import PartitionSpec as P

D = 1152
ROWS = 128
CAPS_HERE = 48
TOKENS = 6
NORM_EPS = 1e-06
HALF = 640
FAN = 8
PIECES = 2
PIECE = ROWS // PIECES
PEER, CROSS, FAR = 5, 5, 8
FAR_FIRST = (4, 3, 5, 2, 6, 1, 7)
MESH = pl.DeviceIdType.MESH
BF16 = jnp.bfloat16
F32 = jnp.float32


def iota(shape, dim):
    return lax.broadcasted_iota(jnp.int32, shape, dim)


def dot(a, b):
    return lax.dot_general(a, b, (((1,), (0,)), ((), ())), preferred_element_type=F32)


def dot_t(a, b):
    return lax.dot_general(a, b, (((1,), (1,)), ((), ())), preferred_element_type=F32)


def swap_pairs(r):
    return ((r >> 1) & 7) * 16 + (r >> 4) * 2 + (r & 1)


def kernel(
    tokens_hbm,
    lengths_hbm,
    caption_ids_hbm,
    destination_hbm,
    slot_hbm,
    images_hbm,
    image_ids_hbm,
    head_hbm,
    scale_ref,
    bias_ref,
    out_image,
    out_text,
    out_loss,
    tokens,
    meta,
    images,
    image_ids_in,
    head,
    im_buf,
    im_ids,
    tx_buf,
    tx_ids,
    send_a1,
    recv_a1,
    send_a2,
    recv_a2,
    send_b1,
    recv_b1,
    send_b2,
    recv_b2,
    raw_ref,
    image_sum,
    text_sum,
    txp_out,
    txp_in,
    in_sem,
    swap_send,
    swap_recv,
    z_send,
    z_recv,
    zid_send,
    zid_recv,
    x_send,
    x_recv,
):
    blk = lax.axis_index("blk")
    grp = lax.axis_index("group")
    col = blk % 2
    peer = {"blk": blk + 1 - 2 * col}
    up = {"blk": (blk + 2) % 16}
    down = {"blk": (blk + 14) % 16}
    y, u = grp // FAN, grp % FAN
    y_peer = [{"group": ((y + k) % FAN) * FAN + u} for k in range(FAN)]
    u_peer = [{"group": y * FAN + (u + k) % FAN} for k in range(FAN)]

    loads = [
        pltpu.make_async_copy(src, dst, in_sem.at[i])
        for i, (src, dst) in enumerate(
            [
                (lengths_hbm, meta.at[0]),
                (destination_hbm, meta.at[1]),
                (slot_hbm, meta.at[2]),
                (caption_ids_hbm, meta.at[3]),
                (tokens_hbm, tokens),
                (images_hbm, images),
                (image_ids_hbm, image_ids_in),
                (head_hbm, head),
            ]
        )
    ]
    for load in loads[:5]:
        load.start()

    barrier = pltpu.get_barrier_semaphore()
    greeted = [peer, up, down] + y_peer[1:] + u_peer[1:]
    for other in greeted:
        pl.semaphore_signal(barrier, inc=1, device_id=other, device_id_type=MESH)
    for load in loads[5:7]:
        load.start()

    def remote(src, dst, send, recv, to):
        return pltpu.make_async_remote_copy(
            src_ref=src, dst_ref=dst, send_sem=send, recv_sem=recv, device_id=to, device_id_type=MESH
        )

    for i in range(4):
        loads[i].wait()
    lengths = meta[0]
    position = meta[1] * 2 + meta[2]
    places = 288
    spread = iota((CAPS_HERE, places), 1) - iota((CAPS_HERE, places), 0)
    hit = spread == 0
    level = jnp.zeros((1, places), jnp.int32)
    lane = iota((1, places), 1)
    for step in range(1, TOKENS):
        hit = hit | (spread == CAPS_HERE * step)
        level = level + (lane >= CAPS_HERE * step).astype(jnp.int32)
    spread_b = hit.astype(F32).astype(BF16)
    wide_length = dot(jnp.broadcast_to(lengths, (16, CAPS_HERE)).astype(F32).astype(BF16), spread_b)[0:1, :]
    wide_position = dot(jnp.broadcast_to(position, (16, CAPS_HERE)).astype(F32).astype(BF16), spread_b)[0:1, :]
    wide_position = jnp.where(level.astype(F32) < wide_length, wide_position, -1.0)

    def row_slot(r):
        return ((y + (r >> 4)) % FAN) * 16 + ((u + ((r >> 1) & 7)) % FAN) * 2 + (r & 1)

    def gather_matrix(order):
        return (order.astype(F32) == wide_position).astype(F32).astype(BF16)

    def own_captions(order):
        return order == position

    loads[4].wait()
    loads[7].start()
    order_a = row_slot(iota((ROWS, 1), 0))
    order_b = row_slot(swap_pairs(iota((ROWS, 1), 0)))
    here_a = own_captions(order_a)
    here_b = own_captions(order_b)
    count_a = jnp.sum(jnp.where(here_a, lengths, 0).astype(F32), axis=1, keepdims=True)
    count_b = jnp.sum(jnp.where(here_b, lengths, 0).astype(F32), axis=1, keepdims=True)
    ids_b = jnp.sum(jnp.where(here_b, meta[3] + 1, 0).astype(F32), axis=1, keepdims=True).astype(jnp.int32)
    send_a1[...] = (dot(gather_matrix(order_a), tokens[:, 0:HALF]) / jnp.maximum(count_a, 1.0)).astype(BF16)
    send_b1[:, 0 : D - HALF] = (
        dot(gather_matrix(order_b), tokens[:, HALF:D]) / jnp.maximum(count_b, 1.0)
    ).astype(BF16)
    id_lane = iota((ROWS, ROWS), 1)
    send_b1[:, D - HALF : HALF] = (
        jnp.where(id_lane == 0, ids_b >> 5, jnp.where(id_lane == 1, ids_b & 31, 0)).astype(F32).astype(BF16)
    )

    pl.semaphore_wait(barrier, len(greeted))

    def swap(stages):
        for k in FAR_FIRST:
            for stage, src, dst, to in stages:
                rows = pl.ds(k * 16, 16)
                remote(src.at[rows], dst.at[rows], swap_send.at[stage], swap_recv.at[stage], to[k]).start()
        alls = []
        for stage, src, dst, to in stages:
            dst[0:16, :] = src[0:16, :]
            rows = pl.ds(16, ROWS - 16)
            alls.append([remote(src.at[rows], dst.at[rows], swap_send.at[stage], swap_recv.at[stage], to[1])])
        return alls

    ways = ((up, 1), (down, 2))

    def start_piece(kind, buf, piece, start=0, land=0):
        copies = []
        for to, place in ways:
            copy = remote(
                buf.at[pl.ds(start * ROWS + piece * PIECE, PIECE)],
                buf.at[pl.ds((land + place) * ROWS + piece * PIECE, PIECE)],
                z_send.at[kind, place, piece],
                z_recv.at[kind, place, piece],
                to,
            )
            copy.start()
            copies.append(copy)
        return copies

    def start_ids(kind, ids, start=0, land=0):
        copies = []
        for to, place in ways:
            copy = remote(
                ids.at[start], ids.at[land + place], zid_send.at[kind, place], zid_recv.at[kind, place], to
            )
            copy.start()
            copies.append(copy)
        return copies

    def own_along_z(kind, buf, ids):
        copies = []
        for piece in range(PIECES):
            copies += start_piece(kind, buf, piece)
        return copies + start_ids(kind, ids)

    def pass_piece(kind, buf, arriving, piece):
        copies = []
        for way, (to, place) in enumerate(ways):
            arriving[piece * 2 + way].wait_recv()
            far = place + 2
            copy = remote(
                buf.at[pl.ds(place * ROWS + piece * PIECE, PIECE)],
                buf.at[pl.ds(far * ROWS + piece * PIECE, PIECE)],
                z_send.at[kind, far, piece],
                z_recv.at[kind, far, piece],
                to,
            )
            copy.start()
            copies.append(copy)
        return copies

    def pass_ids(kind, ids, arriving):
        copies = []
        for way, (to, place) in enumerate(ways):
            arriving[PIECES * 2 + way].wait_recv()
            far = place + 2
            copy = remote(ids.at[place], ids.at[far], zid_send.at[kind, far], zid_recv.at[kind, far], to)
            copy.start()
            copies.append(copy)
        return copies

    def to_peer(i, src, dst):
        copy = remote(src, dst, x_send.at[i], x_recv.at[i], peer)
        copy.start()
        return copy

    swap_a1, swap_b1 = swap([(0, send_a1, recv_a1, y_peer), (1, send_b1, recv_b1, u_peer)])

    loads[5].wait()
    loads[6].wait()
    image_f = images[...].astype(F32)
    image_factor = lax.rsqrt(jnp.sum(image_f * image_f, axis=1, keepdims=True) + NORM_EPS)
    im_buf[0:ROWS, :] = (image_f * image_factor).astype(BF16)
    im_ids[0] = jnp.broadcast_to(image_ids_in[...].astype(F32), (8, ROWS))
    im_near = own_along_z(0, im_buf, im_ids)

    r_out = iota((ROWS, ROWS), 0)
    r_in = iota((ROWS, ROWS), 1)
    turn = (swap_pairs(r_out) == r_in).astype(F32).astype(BF16)
    for copy in swap_a1:
        copy.wait_recv()
    send_a2[...] = dot(turn, recv_a1[...]).astype(BF16)
    (swap_a2,) = swap([(2, send_a2, recv_a2, u_peer)])
    for copy in swap_b1:
        copy.wait_recv()
    send_b2[...] = dot(turn, recv_b1[...]).astype(BF16)
    (swap_b2,) = swap([(3, send_b2, recv_b2, y_peer)])

    im_far = []
    for piece in range(PIECES):
        im_far += pass_piece(0, im_buf, im_near, piece)
    im_far += pass_ids(0, im_ids, im_near)

    def home_slot(r):
        return ((y + FAN - (r >> 4)) % FAN) * 16 + ((u + FAN - ((r >> 1) & 7)) % FAN) * 2 + (r & 1)

    home = (home_slot(r_in) == r_out).astype(F32).astype(BF16)
    for copy in swap_a2:
        copy.wait_recv()
    pooled_a = dot(turn, recv_a2[...]).astype(BF16)
    loads[7].wait()
    raw_a = dot(pooled_a, head[0:HALF, :])
    for copy in swap_b2:
        copy.wait_recv()
    raw = raw_a + dot(recv_b2[:, 0 : D - HALF], head[HALF:D, :])
    text_factor = lax.rsqrt(jnp.sum(raw * raw, axis=1, keepdims=True) + NORM_EPS)
    tx_near, tx_x = [], []
    for piece in range(PIECES):
        rows = pl.ds(piece * PIECE, PIECE)
        top, end = piece * PIECE, (piece + 1) * PIECE
        tx_buf[rows, :] = (raw[top:end, :] * text_factor[top:end, :]).astype(BF16)
        tx_near += start_piece(1, tx_buf, piece)
        tx_x.append(to_peer(piece, tx_buf.at[rows], tx_buf.at[pl.ds(PEER * ROWS + piece * PIECE, PIECE)]))
        if piece > 0:
            continue
        id_codes = recv_b2[:, D - HALF : HALF]
        weigh_in = jnp.where(r_in == 0, 32.0, jnp.where(r_in == 1, 1.0, 0.0)).astype(BF16)
        tx_cols = dot_t(weigh_in, id_codes) - 1.0
        tx_ids[0] = tx_cols[0:8, :]
        tx_near_ids = start_ids(1, tx_ids)
        tx_x_ids = to_peer(2, tx_ids.at[0], tx_ids.at[PEER])
    tx_near += tx_near_ids
    tx_x.append(tx_x_ids)
    raw_ref[...] = raw

    scale = scale_ref[0]
    bias = bias_ref[0]

    def as_rows(ids):
        return jnp.transpose(jnp.broadcast_to(ids, (ROWS, ROWS)))

    def terms(rows, row_ids, cols, col_ids, text_is_rows, far_masks):
        logits = scale * dot_t(rows, cols) + bias
        blocks = len(col_ids)
        wide_cols = jnp.concatenate(col_ids, axis=1)
        wide_rows = jnp.concatenate([row_ids] * blocks, axis=1)
        same = wide_rows == wide_cols
        live = ((wide_rows if text_is_rows else wide_cols) >= 0.0).astype(F32)
        if far_masks is not None:
            ones = jnp.ones((1, ROWS), F32)
            allowed = jnp.concatenate(
                [ones] * (blocks - 2) + [ones * far_masks[0], ones * far_masks[1]], axis=1
            )
            live = live * allowed
        flipped = jnp.where(same, -logits, logits)
        small = jnp.exp(-jnp.abs(flipped))
        sigmoid = jnp.where(flipped >= 0.0, 1.0, small) / (1.0 + small)
        weights = (live * jnp.where(same, -scale, scale) * sigmoid).astype(BF16)
        if text_is_rows:
            return weights, None
        softplus = jnp.maximum(flipped, 0.0) + jnp.log1p(small)
        return weights, jnp.sum(live * softplus, axis=1, keepdims=True)

    col_f = col.astype(F32)
    far_masks = (col_f, 1.0 - col_f)

    im_rows = as_rows(im_ids[0][0:1, :])

    tx_far, tx_cross, txp = [], [], []
    for piece in range(PIECES):
        tx_far += pass_piece(1, tx_buf, tx_near, piece)
        tx_x[piece].wait_recv()
        if piece == 0:
            for copy in im_far:
                copy.wait_recv()
            im_cols = [im_ids[place][0:1, :] for place in range(5)]
            tx_x[PIECES].wait_recv()
            peer_rows = as_rows(tx_ids[PEER][0:1, :])
        if piece == PIECES - 1:
            for part in range(PIECES):
                tx_cross += start_piece(2, tx_buf, part, PEER, CROSS)
            tx_cross += start_ids(2, tx_ids, PEER, CROSS)
            tx_far += pass_ids(1, tx_ids, tx_near)
        top, end = piece * PIECE, (piece + 1) * PIECE
        peer_text = tx_buf[PEER * ROWS + top : PEER * ROWS + end, :]
        weights, _ = terms(peer_text, peer_rows[top:end, :], im_buf[...], im_cols, True, far_masks)
        txp_out[top:end, :] = dot(weights, im_buf[...]).astype(BF16)
        txp.append(to_peer(3 + piece, txp_out.at[pl.ds(top, PIECE)], txp_in.at[pl.ds(top, PIECE)]))

    weights, _ = terms(tx_buf[0:ROWS, :], as_rows(tx_cols[0:1, :]), im_buf[...], im_cols, True, None)
    text_sum[...] = dot(weights, im_buf[...])

    def image_terms(place, blocks):
        cols = tx_buf[place * ROWS : (place + blocks) * ROWS, :]
        ids = [tx_ids[p][0:1, :] for p in range(place, place + blocks)]
        weights, loss = terms(im_buf[0:ROWS, :], im_rows, cols, ids, False, None)
        return dot(weights, cols), loss

    part, loss_own = image_terms(0, 3)
    image_sum[...] = part
    part, loss = image_terms(PEER, 1)
    image_sum[...] += part
    loss_own = loss_own + loss

    lacking = 4 - col
    tx_last = []
    for piece in range(PIECES):
        for way in range(2):
            tx_far[piece * 2 + way].wait_recv()
        tx_last.append(
            to_peer(
                5 + piece,
                tx_buf.at[pl.ds(pl.multiple_of(lacking * ROWS + piece * PIECE, PIECE), PIECE)],
                tx_buf.at[pl.ds(FAR * ROWS + piece * PIECE, PIECE)],
            )
        )
    for way in range(2):
        tx_far[PIECES * 2 + way].wait_recv()
    tx_last.append(to_peer(7, tx_ids.at[lacking], tx_ids.at[FAR]))
    part, loss = image_terms(3, 2)
    image_sum[...] += part
    loss_own = loss_own + loss

    for copy in txp:
        copy.wait_recv()
    total = text_sum[...] + txp_in[...].astype(F32)
    text_norm = raw_ref[...] * text_factor
    along = jnp.sum(text_norm * total, axis=1, keepdims=True)
    text_raw_grad = (text_factor * (total - text_norm * along)).astype(BF16)
    out_text[...] = dot_t(dot(home, text_raw_grad).astype(BF16), head[...])

    for copy in swap_a1 + swap_b1 + swap_a2 + swap_b2 + im_near + im_far:
        copy.wait_send()
    for copy in tx_near + tx_x + txp + tx_far + tx_cross + tx_last:
        copy.wait_send()

    for copy in tx_cross + tx_last:
        copy.wait_recv()
    part, loss = image_terms(CROSS + 1, 3)
    loss_own = loss_own + loss
    total = image_sum[...] + part
    image_norm = images[...].astype(F32) * image_factor
    along = jnp.sum(image_norm * total, axis=1, keepdims=True)
    out_image[...] = image_factor * (total - image_norm * along)
    out_loss[...] = jnp.transpose(jnp.broadcast_to(loss_own, (ROWS, ROWS)))[0:1, :]


def settle(image_in, text_in, loss_in, image_out, text_out, loss_out, sem):
    copies = [
        pltpu.make_async_copy(src, dst, sem.at[i])
        for i, (src, dst) in enumerate(((image_in, image_out), (text_in, text_out), (loss_in, loss_out)))
    ]
    for copy in copies:
        copy.start()
    for copy in copies:
        copy.wait()


def per_device(
    tokens, lengths, caption_ids, destination, slot, images, image_ids, head_weight, logit_scale, logit_bias
):
    any_spec = pl.BlockSpec(memory_space=pl.ANY)
    vmem_spec = pl.BlockSpec(memory_space=pltpu.VMEM)
    smem_spec = pl.BlockSpec(memory_space=pltpu.SMEM)

    def vmem(shape, dtype):
        return pltpu.VMEM(shape, dtype)

    block = (ROWS, D)
    flat_tokens = jnp.transpose(tokens, (1, 0, 2)).reshape(TOKENS * CAPS_HERE, D)
    as_row = lambda a: a.reshape(1, a.shape[0])
    image_grad, text_grad, loss = pl.pallas_call(
        kernel,
        out_shape=(pltpu.VMEM(block, F32), pltpu.VMEM(block, F32), pltpu.VMEM((1, ROWS), F32)),
        in_specs=[any_spec] * 8 + [smem_spec] * 2,
        out_specs=(vmem_spec,) * 3,
        scratch_shapes=[
            vmem((TOKENS * CAPS_HERE, D), BF16),
            vmem((4, 1, CAPS_HERE), jnp.int32),
            vmem(block, BF16),
            vmem((1, ROWS), jnp.int32),
            vmem((D, D), BF16),
            vmem((5 * ROWS, D), BF16),
            vmem((5, 8, ROWS), F32),
            vmem((9 * ROWS, D), BF16),
            vmem((9, 8, ROWS), F32),
        ]
        + [vmem((ROWS, HALF), BF16)] * 8
        + [
            vmem(block, F32),
            vmem(block, F32),
            vmem(block, F32),
            vmem(block, BF16),
            vmem(block, BF16),
            pltpu.SemaphoreType.DMA((8,)),
            pltpu.SemaphoreType.DMA((4,)),
            pltpu.SemaphoreType.DMA((4,)),
            pltpu.SemaphoreType.DMA((3, 5, PIECES)),
            pltpu.SemaphoreType.DMA((3, 5, PIECES)),
            pltpu.SemaphoreType.DMA((3, 5)),
            pltpu.SemaphoreType.DMA((3, 5)),
            pltpu.SemaphoreType.DMA((8,)),
            pltpu.SemaphoreType.DMA((8,)),
        ],
        compiler_params=pltpu.CompilerParams(
            collective_id=0, has_side_effects=True, vmem_limit_bytes=40 * 1024 * 1024
        ),
        name="band",
    )(
        *[
            pltpu.with_memory_space_constraint(a, pltpu.HBM)
            for a in (
                flat_tokens,
                as_row(lengths),
                as_row(caption_ids),
                as_row(destination),
                as_row(slot),
                images,
                as_row(image_ids),
                head_weight,
            )
        ],
        logit_scale,
        logit_bias,
    )
    image_grad, text_grad, loss = pl.pallas_call(
        settle,
        out_shape=(
            jax.ShapeDtypeStruct(block, F32),
            jax.ShapeDtypeStruct(block, F32),
            jax.ShapeDtypeStruct((1, ROWS), F32),
        ),
        in_specs=[vmem_spec] * 3,
        out_specs=(any_spec, any_spec, any_spec),
        scratch_shapes=[pltpu.SemaphoreType.DMA((3,))],
        compiler_params=pltpu.CompilerParams(vmem_limit_bytes=40 * 1024 * 1024),
        name="settle",
    )(image_grad, text_grad, loss)
    return (image_grad, text_grad, loss.reshape(ROWS))


def solution(mesh):
    spec1 = P(("blk", "group"))
    spec2 = P(("blk", "group"), None)
    return jax.shard_map(
        per_device,
        mesh=mesh,
        in_specs=(
            P(("blk", "group"), None, None),
            spec1,
            spec1,
            spec1,
            spec1,
            spec2,
            spec1,
            P(None, None),
            P(None),
            P(None),
        ),
        out_specs=(spec2, spec2, spec1),
        check_vma=False,
    )
```
